128 devices in a mesh: pipe: 4 (over y_hi, core), fsdp: 32 (over x, z, y_lo).
Axes of the slice: x: 4, y: 4 (y_hi: 2, y_lo: 2; y = y_hi * 2 + y_lo), z: 4, core: 2. Of those that a mesh axis runs over, the one named last changes fastest.
Arguments:
- inputs: bfloat16 [4, 2048, 8192], P(None, 'fsdp'), may hold values from -60 to 60
- cotangent: bfloat16 [4, 2048, 8192], P(None, 'fsdp'), may hold values from -0.25 to 0.25
- right_factor: bfloat16 [4, 64, 128, 128], P('pipe', 'fsdp'), may hold values from -0.5 to 0.5
- left_factor: bfloat16 [4, 64, 128, 128], P('pipe', 'fsdp'), may hold values from -0.5 to 0.5
- norm_gain: bfloat16 [4, 8192], P('pipe', 'fsdp'), may hold values from 0.25 to 1.75
Outputs:
- grad_right: float32 [4, 64, 128, 128], P('pipe', 'fsdp')
- grad_left: float32 [4, 64, 128, 128], P('pipe', 'fsdp')
- grad_gain: float32 [4, 8192], P('pipe', 'fsdp')
The draws below stay inside these ranges and needn't reach their ends.
All inputs are finite; a program needn't handle non-finite values.
Results may differ from the reference program's by a relative error of at most 0.034.
Values may be sent and summed in bfloat16 or wider, within the bound.
No kernel may reach another device: no remote copies, remote signals or barrier semaphores. Data moves between devices by JAX's collectives and lax.ppermute only.
A program may use at most 192 MiB of HBM per device.

```python
import jax
import jax.numpy as jnp
from jax import lax

NB = 64
BS = 128
D = 8192
MICRO = 4
MB_TOK = 64
LAYERS = 4
TOKENS = 2048
N_FSDP = 32


def draw_inputs(key, part):
    key_list = jax.random.split(key, 3)
    row_scale = jnp.exp(jax.random.uniform(key_list[1], (MICRO, TOKENS, 1), jnp.float32, -1.2, 1.2))
    column_scale = jnp.exp(jax.random.uniform(key_list[2], (1, 1, D), jnp.float32, -1.2, 1.2))
    base_draw = jnp.clip(jax.random.normal(key_list[0], (MICRO, TOKENS, D), jnp.float32), -5.0, 5.0)
    return (base_draw * row_scale * column_scale).astype(jnp.bfloat16)


def shard_levels(rng, extent, cuts, least, top_value):
    loudness = 1.0
    for dim, parts in cuts:
        draws = jax.random.uniform(jax.random.fold_in(jax.random.fold_in(rng, 6), dim), (parts,), jnp.float32, least / len(cuts), top_value / len(cuts))
        loudness = loudness * jnp.repeat(jnp.exp(draws), extent[dim] // parts).reshape((-1,) + (1,) * (len(extent) - 1 - dim))
    return loudness


def scatter_about(own_key, extent, width, most, cuts=(), held_as=jnp.bfloat16):
    gain = shard_levels(own_key, extent, cuts, -0.22, 0.18) if cuts else 1.0
    entries = jax.random.normal(own_key, extent, jnp.float32) * width * gain
    return jnp.minimum(jnp.maximum(entries, -most), most).astype(held_as)


def setup_inputs(seed: int = 0) -> dict:
    keys = jax.random.split(jax.random.key(seed), 6)
    return {
        "inputs": draw_inputs(jax.random.fold_in(keys[5], 71), 0),
        "cotangent": scatter_about(keys[1], (MICRO, TOKENS, D), (1.5 / (MICRO * MB_TOK * N_FSDP) ** 0.5), 0.25, ((1, 32),)),
        "right_factor": scatter_about(keys[2], (LAYERS, NB, BS, BS), BS ** -0.5, 0.5, ((0, 4), (1, 32))),
        "left_factor": scatter_about(keys[3], (LAYERS, NB, BS, BS), BS ** -0.5, 0.5, ((0, 4), (1, 32))),
        "norm_gain": jnp.clip(1.0 + 0.15 * jax.random.normal(keys[4], (LAYERS, D), jnp.float32), 0.25, 1.75).astype(jnp.bfloat16),
    }


EPSILON = 1e-05
TANH_SLOPE = 0.7978845608028654
CUBIC_TERM = 0.044715
HIGHEST = lax.Precision.HIGHEST

def rounded(array_in):
    return lax.optimization_barrier(array_in.astype(jnp.bfloat16)).astype(jnp.float32)

def gelu_value(pre_act):
    return 0.5 * pre_act * (1.0 + jnp.tanh(TANH_SLOPE * (pre_act + CUBIC_TERM * pre_act * pre_act * pre_act)))

def gelu_slope(pre_act):
    inner_tanh = jnp.tanh(TANH_SLOPE * (pre_act + CUBIC_TERM * pre_act * pre_act * pre_act))
    return 0.5 * (1.0 + inner_tanh) + 0.5 * pre_act * (1.0 - inner_tanh * inner_tanh) * TANH_SLOPE * (1.0 + 3.0 * CUBIC_TERM * pre_act * pre_act)

def layer_parts(float_in, gain_row, right_blocks, left_blocks):
    row_count = float_in.shape[0]
    blocks = right_blocks.shape[0]
    block_size = right_blocks.shape[1]
    share_size = block_size // blocks
    rms_scale = lax.rsqrt(lax.optimization_barrier(jnp.mean(float_in * float_in, axis=-1, keepdims=True)) + EPSILON)
    normed = rounded(float_in * rms_scale * gain_row)
    first_out = rounded(jnp.einsum('tkc,kcd->tkd', normed.reshape(row_count, blocks, block_size), right_blocks, precision=HIGHEST))
    permuted = first_out.reshape(row_count, blocks, share_size, blocks)
    left_four = left_blocks.reshape(blocks, blocks, share_size, block_size)
    pre_act = jnp.einsum('tahj,jahd->tjd', permuted, left_four, precision=HIGHEST).reshape(row_count, blocks * block_size)
    return (rms_scale, normed, permuted, left_four, pre_act)

def layer_forward(float_in, gain_row, right_blocks, left_blocks):
    pre_act = layer_parts(float_in, gain_row, right_blocks, left_blocks)[4]
    return rounded(float_in + gelu_value(pre_act))

def layer_back(float_in, gain_row, right_blocks, left_blocks, grad_out):
    rms_scale, normed, permuted, left_four, pre_act = layer_parts(float_in, gain_row, right_blocks, left_blocks)
    row_count = float_in.shape[0]
    blocks = right_blocks.shape[0]
    block_size = right_blocks.shape[1]
    grad_pre = rounded(grad_out * gelu_slope(pre_act)).reshape(row_count, blocks, block_size)
    grad_left = jnp.einsum('tahj,tjd->jahd', permuted, grad_pre, precision=HIGHEST).reshape(blocks, block_size, block_size)
    grad_first = rounded(jnp.einsum('tjd,jahd->tahj', grad_pre, left_four, precision=HIGHEST)).reshape(row_count, blocks, block_size)
    grad_right = jnp.einsum('tkc,tkd->kcd', normed.reshape(row_count, blocks, block_size), grad_first, precision=HIGHEST)
    grad_normed = jnp.einsum('tkd,kcd->tkc', grad_first, right_blocks, precision=HIGHEST).reshape(row_count, blocks * block_size)
    grad_gain = lax.optimization_barrier(jnp.sum(grad_normed * float_in * rms_scale, axis=0))
    weighted = grad_normed * gain_row
    grad_in = rounded(grad_out + rms_scale * weighted - float_in * rms_scale ** 3 * lax.optimization_barrier(jnp.mean(weighted * float_in, axis=-1, keepdims=True)))
    return (grad_in, grad_right, grad_left, grad_gain)

def reference(inputs, cotangent, right_factor, left_factor, norm_gain):
    micro_count, token_count, feature_width = inputs.shape

    def by_device(array_in):
        shaped = array_in.astype(jnp.float32).reshape(micro_count, N_FSDP, MB_TOK, feature_width)
        return shaped.transpose(1, 0, 2, 3).reshape(N_FSDP, micro_count * MB_TOK, feature_width)
    rights = right_factor.astype(jnp.float32)
    lefts = left_factor.astype(jnp.float32)
    gains = norm_gain.astype(jnp.float32)

    def one_device(totals, row_pair):
        act_rows, grad_rows = row_pair
        layer_inputs = [act_rows]
        for layer in range(LAYERS - 1):
            layer_inputs.append(layer_forward(layer_inputs[-1], gains[layer], rights[layer], lefts[layer]))
        pieces_right = [None] * LAYERS
        pieces_left = [None] * LAYERS
        pieces_gain = [None] * LAYERS
        grad_now = grad_rows
        for layer in reversed(range(LAYERS)):
            grad_now, piece_right, piece_left, piece_gain = layer_back(layer_inputs[layer], gains[layer], rights[layer], lefts[layer], grad_now)
            pieces_right[layer] = piece_right
            pieces_left[layer] = piece_left
            pieces_gain[layer] = piece_gain
        new_totals = (totals[0] + rounded(jnp.stack(pieces_right)), totals[1] + rounded(jnp.stack(pieces_left)), totals[2] + rounded(jnp.stack(pieces_gain)))
        return (new_totals, None)
    start_totals = (jnp.zeros(right_factor.shape, jnp.float32), jnp.zeros(left_factor.shape, jnp.float32), jnp.zeros(norm_gain.shape, jnp.float32))
    final_totals, unused = lax.scan(one_device, start_totals, (by_device(inputs), by_device(cotangent)))
    return (final_totals[0], final_totals[1], final_totals[2])
```

```python
import functools

import jax
import jax.numpy as jnp
from jax import lax
from jax.experimental import pallas as pl
from jax.experimental.pallas import tpu as pltpu
from jax.sharding import Mesh, PartitionSpec as P

EPSILON = 1e-05
TANH_SLOPE = 0.7978845608028654
CUBIC_TERM = 0.044715

BF = jnp.bfloat16
F32 = jnp.float32
HI = lax.Precision.HIGHEST
SWAP = ((0, 1), (1, 0))
XZ = ("x", "z")
VMEM_LIMIT = 56 * 1024 * 1024

NB = 64
BS = 128
D = NB * BS
HB = NB // 2
ROWS = HB * BS
HALF = ROWS // 2
TOK = 128
STAT = 16
GRID = 4
BPC = HB // GRID


def mm(a, b):
    return lax.dot_general(a, b, (((1,), (0,)), ((), ())), preferred_element_type=F32)


def mm_ta(a, b):
    return lax.dot_general(a, b, (((0,), (0,)), ((), ())), preferred_element_type=F32)


def mm_tb(a, b):
    return lax.dot_general(a, b, (((1,), (1,)), ((), ())), preferred_element_type=F32)


def iota2(dim):
    return lax.broadcasted_iota(jnp.int32, (BS, BS), dim)


def column_source(dp, q):
    rel = dp // 64
    return ((dp // 32) % 2) * 64 + 2 * (dp % 32) + (rel + q - 2 * rel * q)


def row_source(cp, q):
    rel = cp // 64
    return 4 * ((cp % 64) // 2) + 2 * (rel + q - 2 * rel * q) + cp % 2


def stat_rows(value):
    hi = value.astype(BF)
    rest = value - hi.astype(F32)
    mid = rest.astype(BF)
    lo = (rest - mid.astype(F32)).astype(BF)
    row = lax.broadcasted_iota(jnp.int32, (STAT, TOK), 0)
    out = jnp.where(row == 0, hi.astype(F32), jnp.where(row == 1, mid.astype(F32), lo.astype(F32)))
    return jnp.where(row < 3, out, 0.0).astype(BF)


def stat_total(own_ref, recv_ref):
    rows = recv_ref[pl.ds(HALF, STAT), :].astype(F32)
    return own_ref[0:1, :] + jnp.sum(rows, axis=0, keepdims=True)


def folded(value):
    return jnp.sum(value.reshape(BS // 8, 8, TOK), axis=0)


def fold_block(ref, i):
    return ref[i // 2, i % 2]


def prep_kernel(core_ref, right_ref, left_ref, gain_ref, keep_ref, send_ref):
    core = core_ref[0]
    for dst, q in ((keep_ref, core), (send_ref, 1 - core)):
        gain_row = gain_ref[q].astype(F32)
        diag = jnp.where(iota2(0) == iota2(1), gain_row, 0.0).astype(BF)
        scaled = mm(diag, right_ref[q]).astype(BF)
        pick = (iota2(0) == column_source(iota2(1), q)).astype(F32).astype(BF)
        dst[0] = mm(scaled, pick).astype(BF)
        pick = (iota2(1) == row_source(iota2(0), q)).astype(F32).astype(BF)
        dst[1] = mm(pick, left_ref[q]).astype(BF)


def put_forward(scr, pair, product):
    for part in range(2):
        for h in range(2):
            scr[part, pl.ds(pair * 2 + h, 32, stride=64), :] = product[part * 64 + h * 32 :][:32]


def put_backward(scr, pair, product):
    for part in range(2):
        scr[part, pl.ds(pair, 64, stride=32), :] = product[part * 64 :][:64]


def flush(scr, acc, own_ref, send_ref, stat_ref):
    @pl.when(pl.program_id(0) == GRID - 1)
    def _():
        own_ref[...] = scr[0].astype(BF)
        send_ref[pl.ds(0, HALF), :] = scr[1].astype(BF)
        total = jnp.sum(acc[...], axis=0, keepdims=True)
        send_ref[pl.ds(HALF, STAT), :] = stat_rows(total)
        stat_ref[...] = jnp.broadcast_to(total, stat_ref.shape)


def clear(acc):
    @pl.when(pl.program_id(0) == 0)
    def _():
        acc[...] = jnp.zeros_like(acc)


def tokens_last(ref, i, core):
    start = pl.multiple_of((2 * i + core) * BS, BS)
    rows = ref[:, :, pl.ds(start, BS)].reshape(TOK, BS)
    return rows.astype(F32).T


def start_kernel(place_ref, in_ref, w_ref, x_ref, own_ref, send_ref, stat_ref, scr, acc):
    core = place_ref[0]
    clear(acc)
    base = pl.program_id(0) * BPC
    for i in range(BPC):
        x = tokens_last(in_ref, i, core)
        xb = x.astype(BF)
        x_ref[pl.ds(i * BS, BS), :] = xb
        acc[...] += folded(x * x)
        put_forward(scr, base + i, mm_ta(fold_block(w_ref, i), xb))
    flush(scr, acc, own_ref, send_ref, stat_ref)


def gelu_parts(v):
    sq = v * v
    t = jnp.tanh(v * (TANH_SLOPE + (TANH_SLOPE * CUBIC_TERM) * sq))
    half = 0.5 * t + 0.5
    slope = half + (v * (1.0 - t * t)) * (0.5 * TANH_SLOPE + (1.5 * TANH_SLOPE * CUBIC_TERM) * sq)
    return v * half, slope


def rms_of(own_stat, recv_ref):
    return lax.rsqrt(stat_total(own_stat, recv_ref) * (1.0 / D) + EPSILON)


def permuted_block(own_ref, recv_ref, pair, rms):
    start = pl.multiple_of(pair * 64, 64)
    both = jnp.concatenate([own_ref[pl.ds(start, 64), :], recv_ref[pl.ds(start, 64), :]], axis=0)
    if rms is None:
        return both
    return (both.astype(F32) * rms).astype(BF)


def forward_kernel(
    uo_ref, ur_ref, us_ref, x_ref, left_ref, w_ref,
    xn_ref, slope_ref, perm_ref, rms_ref, own_ref, send_ref, stat_ref, scr, acc,
):
    clear(acc)
    base = pl.program_id(0) * BPC
    rms = rms_of(us_ref, ur_ref)
    rms_ref[...] = jnp.broadcast_to(rms, rms_ref.shape)
    for i in range(BPC):
        rows = pl.ds(i * BS, BS)
        perm = permuted_block(uo_ref, ur_ref, base + i, rms)
        perm_ref[rows, :] = perm
        value, slope = gelu_parts(mm_ta(fold_block(left_ref, i), perm))
        slope_ref[rows, :] = slope.astype(BF)
        xb = (x_ref[rows, :].astype(F32) + value).astype(BF)
        xn_ref[rows, :] = xb
        x = xb.astype(F32)
        acc[...] += folded(x * x)
        put_forward(scr, base + i, mm_ta(fold_block(w_ref, i), xb))
    flush(scr, acc, own_ref, send_ref, stat_ref)


def left_backward(grad, slope, perm, left, rms, pair, scr, acc):
    grad_pre = (grad.astype(F32) * slope).astype(BF)
    grad_left = mm_tb(perm, grad_pre).astype(BF)
    grad_perm = mm(left, grad_pre)
    acc[...] += folded(grad_perm * perm.astype(F32))
    put_backward(scr, pair, grad_perm * rms)
    return grad_left


def turn_kernel(
    place_ref, uo_ref, ur_ref, us_ref, cot_ref, left_ref,
    grad_ref, rms_ref, gl_ref, own_ref, send_ref, stat_ref, scr, acc,
):
    core = place_ref[0]
    clear(acc)
    base = pl.program_id(0) * BPC
    rms = rms_of(us_ref, ur_ref)
    rms_ref[...] = jnp.broadcast_to(rms, rms_ref.shape)
    for i in range(BPC):
        perm = permuted_block(uo_ref, ur_ref, base + i, rms)
        left = fold_block(left_ref, i)
        slope = gelu_parts(mm_ta(left, perm))[1]
        grad = tokens_last(cot_ref, i, core).astype(BF)
        grad_ref[pl.ds(i * BS, BS), :] = grad
        gl_ref[i // 2, i % 2] = left_backward(grad, slope, perm, left, rms, base + i, scr, acc)
    flush(scr, acc, own_ref, send_ref, stat_ref)


def backward_kernel(
    buf_ref, go_ref, gr_ref, gs_ref, rms_ref, rms_below_ref, x_ref, grad_ref, slope_ref, perm_ref, w_ref, left_ref,
    new_ref, out_ref, own_ref, send_ref, stat_ref, scr, acc,
):
    del buf_ref
    clear(acc)
    base = pl.program_id(0) * BPC
    rms = rms_ref[0:1, :]
    rms_below = rms_below_ref[0:1, :]
    coef = stat_total(gs_ref, gr_ref) * (rms * rms * (1.0 / D))
    for i in range(BPC):
        rows = pl.ds(i * BS, BS)
        gf = permuted_block(go_ref, gr_ref, base + i, None)
        x = x_ref[rows, :]
        out_ref[i // 2, i % 2, 0] = mm_tb(x, gf).astype(BF)
        grad = grad_ref[rows, :].astype(F32) + mm(fold_block(w_ref, i), gf) - x.astype(F32) * coef
        grad = grad.astype(BF)
        new_ref[rows, :] = grad
        out_ref[i // 2, i % 2, 1] = left_backward(
            grad, slope_ref[rows, :].astype(F32), perm_ref[rows, :], fold_block(left_ref, i), rms_below, base + i, scr, acc
        )
    flush(scr, acc, own_ref, send_ref, stat_ref)


def last_kernel(buf_ref, go_ref, gr_ref, x_ref, out_ref):
    del buf_ref
    base = pl.program_id(0) * BPC
    for i in range(BPC):
        gf = permuted_block(go_ref, gr_ref, base + i, None)
        out_ref[i // 2, i % 2] = mm_tb(x_ref[pl.ds(i * BS, BS), :], gf).astype(BF)


def sum_kernel(core_ref, part_ref, keep_ref, send_ref):
    core = core_ref[0]
    for dst, i in ((keep_ref, core), (send_ref, 1 - core)):
        for side in range(2):
            dst[side] = (part_ref[0, i, side].astype(F32) + part_ref[1, i, side].astype(F32)) + (
                part_ref[2, i, side].astype(F32) + part_ref[3, i, side].astype(F32)
            )


def finish_kernel(core_ref, keep_ref, recv_ref, right_ref, gain_ref, gr_ref, gl_ref, gg_ref):
    core = core_ref[0]
    for src, q in ((keep_ref, core), (recv_ref, 1 - core)):
        pick = (iota2(1) == column_source(iota2(0), q)).astype(F32)
        raw = lax.dot_general(src[0], pick, (((1,), (0,)), ((), ())), precision=HI, preferred_element_type=F32)
        diag = jnp.where(iota2(0) == iota2(1), gain_ref[q].astype(F32), 0.0)
        gr_ref[q] = lax.dot_general(diag, raw, (((1,), (0,)), ((), ())), precision=HI, preferred_element_type=F32)
        weighted = raw * right_ref[q].astype(F32)
        ones = jnp.ones((8, BS), F32)
        gg_ref[q] = lax.dot_general(
            ones, weighted, (((1,), (1,)), ((), ())), precision=HI, preferred_element_type=F32
        )[0:1]
        pick = (iota2(0) == row_source(iota2(1), q)).astype(F32)
        gl_ref[q] = lax.dot_general(pick, src[1], (((1,), (0,)), ((), ())), precision=HI, preferred_element_type=F32)


def full(shape):
    return pl.BlockSpec(shape, lambda g, *_: (0,) * len(shape))


ACT = pl.BlockSpec((BPC * BS, TOK), lambda g, *_: (g, 0))
ANY = pl.BlockSpec(memory_space=pl.ANY)
U_SHAPES = (
    jax.ShapeDtypeStruct((HALF, TOK), BF),
    jax.ShapeDtypeStruct((HALF + STAT, TOK), BF),
    jax.ShapeDtypeStruct((8, TOK), F32),
)
U_SPECS = tuple(full(s.shape) for s in U_SHAPES)
ACT_SHAPE = jax.ShapeDtypeStruct((ROWS, TOK), BF)
STAT_SHAPE = jax.ShapeDtypeStruct((8, TOK), F32)
STAT_SPEC = full((8, TOK))
SCRATCH = [pltpu.VMEM((2, HALF, TOK), F32), pltpu.VMEM((8, TOK), F32)]
PARAMS = pltpu.CompilerParams(vmem_limit_bytes=VMEM_LIMIT)


def weight_spec(layer, side):
    return pl.BlockSpec(
        (None, 4, None, 2, None, None, BS, BS), lambda g, *_: (g, 0, layer // 2, 0, layer % 2, side, 0, 0)
    )


TOKENS_SPEC = pl.BlockSpec((2, 64, D // GRID), lambda g, place: (place[1], 0, g))


def call(kernel, ins, in_specs, out_shapes, out_specs, scratch=(), grid=GRID, prefetch=0, aliases=None):
    return pl.pallas_call(
        kernel,
        out_shape=out_shapes,
        grid_spec=pltpu.PrefetchScalarGridSpec(
            num_scalar_prefetch=prefetch, grid=(grid,), in_specs=in_specs, out_specs=out_specs, scratch_shapes=scratch
        ),
        input_output_aliases=aliases or {},
        compiler_params=PARAMS,
    )(*ins)


def swapped(value):
    return lax.ppermute(value, "c", SWAP)


def per_device(inputs, cotangent, right_factor, left_factor, norm_gain):
    core = lax.axis_index("c")
    place = jnp.stack([core, lax.axis_index("yh")]).astype(jnp.int32)
    right = right_factor[0]
    left = left_factor[0]
    gain = norm_gain.reshape(2, 1, BS)
    pair = jax.ShapeDtypeStruct((2, BS, BS), BF)
    keep, send = call(
        prep_kernel, (place, right, left, gain), [full((2, BS, BS))] * 2 + [full((2, 1, BS))],
        (pair, pair), (full((2, BS, BS)),) * 2, grid=1, prefetch=1,
    )
    recv = swapped(send)
    mine = jnp.stack([jnp.where(core == 0, keep, recv), jnp.where(core == 0, recv, keep)])
    weights = lax.all_gather(mine, ("x", "z", "yh", "yl"), axis=0, tiled=False).reshape(4, 4, 2, 2, 2, 2, BS, BS)

    x0, uo, us, st = call(
        start_kernel, (place, inputs, weights), [TOKENS_SPEC, weight_spec(0, 0)],
        (ACT_SHAPE,) + U_SHAPES, (ACT,) + U_SPECS, SCRATCH, prefetch=1,
    )
    xs, slopes, perms, rmss = [x0], [], [], []
    for layer in range(3):
        xn, slope, perm, rms, uo, us, st = call(
            forward_kernel, (uo, swapped(us), st, xs[-1], weights, weights),
            list((U_SPECS)) + [ACT, weight_spec(layer, 1), weight_spec(layer + 1, 0)],
            (ACT_SHAPE, ACT_SHAPE, ACT_SHAPE, STAT_SHAPE) + U_SHAPES, (ACT, ACT, ACT, STAT_SPEC) + U_SPECS, SCRATCH,
        )
        xs.append(xn)
        slopes.append(slope)
        perms.append(perm)
        rmss.append(rms)
    buf_shape = jax.ShapeDtypeStruct((4, 4, 2, 4, 2, BS, BS), BF)

    def single(slot):
        return pl.BlockSpec((None, 4, 2, None, None, BS, BS), lambda g, *_: (g, 0, 0, 0, slot, 0, 0))

    grad, rms, buf, uo, us, st = call(
        turn_kernel, (place, uo, swapped(us), st, cotangent, weights),
        list(U_SPECS) + [TOKENS_SPEC, weight_spec(3, 1)],
        (ACT_SHAPE, STAT_SHAPE, buf_shape) + U_SHAPES, (ACT, STAT_SPEC, single(1)) + U_SPECS, SCRATCH, prefetch=1,
    )
    rmss.append(rms)
    for layer in (3, 2, 1):
        both = pl.BlockSpec(
            (None, 4, 2, None, 2, BS, BS), functools.partial(lambda n, g, *_: (g, 0, 0, n, 0, 0, 0), layer)
        )
        grad, buf, uo, us, st = call(
            backward_kernel,
            (buf, uo, swapped(us), st, rmss[layer], rmss[layer - 1], xs[layer], grad, slopes[layer - 1], perms[layer - 1],
             weights, weights),
            [ANY] + list(U_SPECS) + [STAT_SPEC] * 2 + [ACT] * 4 + [weight_spec(layer, 0), weight_spec(layer - 1, 1)],
            (ACT_SHAPE, buf_shape) + U_SHAPES, (ACT, both) + U_SPECS, SCRATCH, aliases={0: 1},
        )
    buf = call(
        last_kernel, (buf, uo, swapped(us), xs[0]), [ANY] + list(U_SPECS[:2]) + [ACT],
        buf_shape, single(0), aliases={0: 0},
    )
    part = lax.psum_scatter(buf.reshape(16, 2, 4, 2, BS, BS), XZ, scatter_dimension=0, tiled=True)[0]
    rights = part[:, :, 0]
    lefts = jnp.concatenate([part[:, 1:, 1], part[:, :1, 1]], axis=1)
    piece = jnp.stack([rights, lefts], axis=2).reshape(2, 2, 2, 2, BS, BS).transpose(1, 0, 2, 3, 4, 5)
    piece = lax.all_to_all(piece.reshape(4, 2, 2, BS, BS), ("yh", "yl"), 0, 0, tiled=True)
    sums = jax.ShapeDtypeStruct((2, BS, BS), F32)
    keep, send = call(
        sum_kernel, (place, piece), [full((4, 2, 2, BS, BS))], (sums, sums), (full((2, BS, BS)),) * 2, grid=1, prefetch=1,
    )
    grad_right, grad_left, grad_gain = call(
        finish_kernel, (place, keep, swapped(send), right, gain),
        [full((2, BS, BS))] * 3 + [full((2, 1, BS))],
        (sums, sums, jax.ShapeDtypeStruct((2, 1, BS), F32)),
        (full((2, BS, BS)), full((2, BS, BS)), full((2, 1, BS))), grid=1, prefetch=1,
    )
    return grad_right[None], grad_left[None], grad_gain.reshape(1, 2 * BS)


def solution(mesh):
    parts = Mesh(mesh.devices.reshape(2, 2, 4, 4, 2), ("yh", "c", "x", "z", "yl"))
    pipe, fsdp = ("yh", "c"), ("x", "z", "yl")
    return jax.shard_map(
        per_device,
        mesh=parts,
        in_specs=(P(None, fsdp, None), P(None, fsdp, None), P(pipe, fsdp, None, None), P(pipe, fsdp, None, None), P(pipe, fsdp)),
        out_specs=(P(pipe, fsdp, None, None), P(pipe, fsdp, None, None), P(pipe, fsdp)),
        check_vma=False,
    )
```

```python
import functools

import jax
import jax.numpy as jnp
from jax import lax
from jax.experimental import pallas as pl
from jax.experimental.pallas import tpu as pltpu
from jax.sharding import Mesh, PartitionSpec as P

EPSILON = 1e-05
TANH_SLOPE = 0.7978845608028654
CUBIC_TERM = 0.044715

BF = jnp.bfloat16
F32 = jnp.float32
HI = lax.Precision.HIGHEST
SWAP = ((0, 1), (1, 0))
YS = ("yh", "yl")
VMEM_LIMIT = 24 * 1024 * 1024

NB = 64
BS = 128
D = NB * BS
HB = NB // 2
ROWS = HB * BS
HALF = ROWS // 2
TOK = 128
STAT = 16
GRID = 4
BPC = HB // GRID


def mm(a, b):
    return lax.dot_general(a, b, (((1,), (0,)), ((), ())), preferred_element_type=F32)


def mm_ta(a, b):
    return lax.dot_general(a, b, (((0,), (0,)), ((), ())), preferred_element_type=F32)


def mm_tb(a, b):
    return lax.dot_general(a, b, (((1,), (1,)), ((), ())), preferred_element_type=F32)


def mm_exact(a, b, dims=((1,), (0,))):
    return lax.dot_general(a, b, (dims, ((), ())), precision=HI, preferred_element_type=F32)


def iota2(dim):
    return lax.broadcasted_iota(jnp.int32, (BS, BS), dim)


def column_source(dp, q):
    rel = dp // 64
    return ((dp // 32) % 2) * 64 + 2 * (dp % 32) + (rel + q - 2 * rel * q)


def row_source(cp, q):
    rel = cp // 64
    return 4 * ((cp % 64) // 2) + 2 * (rel + q - 2 * rel * q) + cp % 2


def stat_rows(value):
    hi = value.astype(BF)
    rest = value - hi.astype(F32)
    mid = rest.astype(BF)
    lo = (rest - mid.astype(F32)).astype(BF)
    row = lax.broadcasted_iota(jnp.int32, (STAT, TOK), 0)
    out = jnp.where(row == 0, hi.astype(F32), jnp.where(row == 1, mid.astype(F32), lo.astype(F32)))
    return jnp.where(row < 3, out, 0.0).astype(BF)


def stat_total(own_ref, recv_ref):
    rows = recv_ref[pl.ds(HALF, STAT), :].astype(F32)
    return own_ref[0:1, :] + jnp.sum(rows, axis=0, keepdims=True)


def folded(value):
    return jnp.sum(value.reshape(BS // 8, 8, TOK), axis=0)


def back(index, steps):
    return (index + (4 - steps)) % 4


def blocks(place_ref):
    for sx in range(4):
        xm = back(place_ref[2], sx)
        for sz in range(4):
            zm = back(place_ref[3], sz)
            for ym in range(2):
                yield sx, sz, xm, zm, ym, xm * 8 + zm * 2 + ym


def slot(at, yl, k):
    return at * 4 + yl * 2 + k


def rows_of(m):
    return pl.ds(pl.multiple_of(m * BS, BS), BS)


def prep_kernel(place_ref, right_ref, left_ref, gain_ref, keep_ref, send_ref):
    core = place_ref[0]
    for dst, q in ((keep_ref, core), (send_ref, 1 - core)):
        gain_row = gain_ref[q].astype(F32)
        diag = jnp.where(iota2(0) == iota2(1), gain_row, 0.0).astype(BF)
        scaled = mm(diag, right_ref[q]).astype(BF)
        pick = (iota2(0) == column_source(iota2(1), q)).astype(F32).astype(BF)
        dst[0] = mm(scaled, pick).astype(BF)
        pick = (iota2(1) == row_source(iota2(0), q)).astype(F32).astype(BF)
        dst[1] = mm(pick, left_ref[q]).astype(BF)


def gather_y_kernel(place_ref, p0, p1, p2, p3, right_ref, left_ref):
    core = place_ref[0]
    for s, piece in enumerate((p0, p1, p2, p3)):
        y = back(place_ref[4], s)
        for k in range(2):
            layer = (y // 2) * 2 + (core + k) % 2
            right_ref[y % 2, layer] = piece[k, 0]
            left_ref[y % 2, layer] = piece[k, 1]


def gather_pair_kernel(place_ref, r0, r1, r2, r3, l0, l1, l2, l3, ra_ref, rb_ref, la_ref, lb_ref):
    for index, pieces, first, second in ((3, (r0, r1, r2, r3), ra_ref, rb_ref), (2, (l0, l1, l2, l3), la_ref, lb_ref)):
        for s, piece in enumerate(pieces):
            at = back(place_ref[index], s)
            for yl in range(2):
                for k in range(2):
                    first[slot(at, yl, k)] = piece[yl, k]
                    second[slot(at, yl, k)] = piece[yl, 2 + k]


def tokens_kernel(place_ref, in_ref, cot_ref, x_ref, grad_ref, stat_ref):
    core = place_ref[0]
    base = pl.program_id(0) * BPC
    total = jnp.zeros((8, TOK), F32)
    for i in range(BPC):
        lanes = pl.ds(pl.multiple_of((2 * i + core) * BS, BS), BS)
        x = in_ref[:, :, lanes].reshape(TOK, BS).astype(F32).T
        x_ref[rows_of(base + i), :] = x.astype(BF)
        total = total + folded(x * x)
        grad_ref[rows_of(base + i), :] = cot_ref[:, :, lanes].reshape(TOK, BS).astype(F32).T.astype(BF)
    total = jnp.broadcast_to(jnp.sum(total, axis=0, keepdims=True), (8, TOK))

    @pl.when(pl.program_id(0) == 0)
    def _():
        stat_ref[...] = jnp.zeros_like(stat_ref)

    stat_ref[...] += total


def put_forward(scr, m, product):
    for part in range(2):
        for h in range(2):
            scr[part, pl.ds(m * 2 + h, 32, stride=64), :] = product[part * 64 + h * 32 :][:32]


def put_backward(scr, m, product):
    for part in range(2):
        scr[part, pl.ds(m, 64, stride=32), :] = product[part * 64 :][:64]


def flush(scr, total, own_ref, send_ref, stat_ref):
    own_ref[...] = scr[0].astype(BF)
    send_ref[pl.ds(0, HALF), :] = scr[1].astype(BF)
    send_ref[pl.ds(HALF, STAT), :] = stat_rows(total)
    stat_ref[...] = jnp.broadcast_to(total, stat_ref.shape)


def gelu_parts(v):
    sq = v * v
    t = jnp.tanh(v * (TANH_SLOPE + (TANH_SLOPE * CUBIC_TERM) * sq))
    half = 0.5 * t + 0.5
    slope = half + (v * (1.0 - t * t)) * (0.5 * TANH_SLOPE + (1.5 * TANH_SLOPE * CUBIC_TERM) * sq)
    return v * half, slope


def rms_of(own_stat, recv_ref):
    return lax.rsqrt(stat_total(own_stat, recv_ref) * (1.0 / D) + EPSILON)


def permuted_block(own_ref, recv_ref, m, rms):
    rows = pl.ds(pl.multiple_of(m * 64, 64), 64)
    both = jnp.concatenate([own_ref[rows, :], recv_ref[rows, :]], axis=0)
    if rms is None:
        return both
    return (both.astype(F32) * rms).astype(BF)


def start_kernel(k, place_ref, x_ref, st_ref, w0, w1, w2, w3, own_ref, send_ref, stat_ref, scr):
    rights = (w0, w1, w2, w3)
    for sx, sz, xm, zm, ym, m in blocks(place_ref):
        put_forward(scr, m, mm_ta(rights[sx][slot(zm, ym, k)], x_ref[rows_of(m), :]))
    flush(scr, st_ref[0:1, :], own_ref, send_ref, stat_ref)


def forward_kernel(
    slots, place_ref, uo_ref, ur_ref, us_ref, x_ref, l0, l1, l2, l3, w0, w1, w2, w3,
    xn_ref, slope_ref, perm_ref, rms_ref, own_ref, send_ref, stat_ref, scr,
):
    lefts, rights = (l0, l1, l2, l3), (w0, w1, w2, w3)
    rms = rms_of(us_ref, ur_ref)
    rms_ref[...] = jnp.broadcast_to(rms, rms_ref.shape)
    total = jnp.zeros((8, TOK), F32)
    for sx, sz, xm, zm, ym, m in blocks(place_ref):
        rows = rows_of(m)
        perm = permuted_block(uo_ref, ur_ref, m, rms)
        perm_ref[rows, :] = perm
        value, slope = gelu_parts(mm_ta(lefts[sz][slot(xm, ym, slots[0])], perm))
        slope_ref[rows, :] = slope.astype(BF)
        xb = (x_ref[rows, :].astype(F32) + value).astype(BF)
        xn_ref[rows, :] = xb
        x = xb.astype(F32)
        total = total + folded(x * x)
        put_forward(scr, m, mm_ta(rights[sx][slot(zm, ym, slots[1])], xb))
    flush(scr, jnp.sum(total, axis=0, keepdims=True), own_ref, send_ref, stat_ref)


def left_backward(grad, slope, perm, left, rms, m, scr):
    grad_pre = (grad.astype(F32) * slope).astype(BF)
    grad_left = mm_tb(perm, grad_pre).astype(BF)
    grad_perm = mm(left, grad_pre)
    put_backward(scr, m, grad_perm * rms)
    return grad_left, folded(grad_perm * perm.astype(F32))


def turn_kernel(
    k, place_ref, uo_ref, ur_ref, us_ref, grad_ref, l0, l1, l2, l3,
    rms_ref, g0, g1, g2, g3, own_ref, send_ref, stat_ref, scr,
):
    lefts, outs = (l0, l1, l2, l3), (g0, g1, g2, g3)
    rms = rms_of(us_ref, ur_ref)
    rms_ref[...] = jnp.broadcast_to(rms, rms_ref.shape)
    total = jnp.zeros((8, TOK), F32)
    for sx, sz, xm, zm, ym, m in blocks(place_ref):
        perm = permuted_block(uo_ref, ur_ref, m, rms)
        left = lefts[sz][slot(xm, ym, k)]
        slope = gelu_parts(mm_ta(left, perm))[1]
        outs[sz][slot(xm, ym, k)], add = left_backward(grad_ref[rows_of(m), :], slope, perm, left, rms, m, scr)
        total = total + add
    flush(scr, jnp.sum(total, axis=0, keepdims=True), own_ref, send_ref, stat_ref)


def backward_kernel(slots, n_old, *refs):
    refs = refs[n_old:]
    place_ref, go_ref, gr_ref, gs_ref, rms_ref, rms_below_ref, x_ref, grad_ref, slope_ref, perm_ref = refs[:10]
    rights, lefts, new_ref, out_right, out_left = refs[10:14], refs[14:18], refs[18], refs[19:23], refs[23:27]
    own_ref, send_ref, stat_ref, scr = refs[27:]
    rms = rms_ref[0:1, :]
    rms_below = rms_below_ref[0:1, :]
    coef = stat_total(gs_ref, gr_ref) * (rms * rms * (1.0 / D))
    total = jnp.zeros((8, TOK), F32)
    for sx, sz, xm, zm, ym, m in blocks(place_ref):
        rows = rows_of(m)
        gf = permuted_block(go_ref, gr_ref, m, None)
        x = x_ref[rows, :]
        out_right[sx][slot(zm, ym, slots[0])] = mm_tb(x, gf).astype(BF)
        grad = grad_ref[rows, :].astype(F32) + mm(rights[sx][slot(zm, ym, slots[0])], gf) - x.astype(F32) * coef
        grad = grad.astype(BF)
        new_ref[rows, :] = grad
        out_left[sz][slot(xm, ym, slots[1])], add = left_backward(
            grad, slope_ref[rows, :].astype(F32), perm_ref[rows, :], lefts[sz][slot(xm, ym, slots[1])], rms_below, m, scr
        )
        total = total + add
    flush(scr, jnp.sum(total, axis=0, keepdims=True), own_ref, send_ref, stat_ref)


def last_kernel(k, b0, b1, b2, b3, place_ref, go_ref, gr_ref, x_ref, o0, o1, o2, o3):
    del b0, b1, b2, b3
    outs = (o0, o1, o2, o3)
    for sx, sz, xm, zm, ym, m in blocks(place_ref):
        gf = permuted_block(go_ref, gr_ref, m, None)
        outs[sx][slot(zm, ym, k)] = mm_tb(x_ref[rows_of(m), :], gf).astype(BF)


def added(parts):
    a, b, c, d = (p.astype(F32) for p in parts)
    return (a + b) + (c + d)


def sum_slab_kernel(place_ref, a_ref, b_ref, c_ref, d_ref, out_ref):
    del place_ref
    for i in range(16):
        out_ref[i] = added((a_ref[i], b_ref[i], c_ref[i], d_ref[i])).astype(BF)


def sum_pair_kernel(place_ref, *refs):
    sources, outs = refs[:10], refs[10:]
    for side, index in ((0, 3), (1, 2)):
        slabs, ready = sources[side * 5 :][:4], sources[side * 5 + 4]
        for s in range(4):
            at = back(place_ref[index], s)
            for yl in range(2):
                for k in range(2):
                    outs[side * 4 + s][yl, k] = added([t[slot(at, yl, k)] for t in slabs]).astype(BF)
                    outs[side * 4 + s][yl, 2 + k] = ready[slot(at, yl, k)]


def sum_ring_kernel(place_ref, *refs):
    sources, outs = refs[:8], refs[8:]
    for side in range(2):
        slabs = sources[side * 4 :][:4]
        for s in range(4):
            y = back(place_ref[4], s)
            for k in range(2):
                outs[s][k, side] = added([t[y % 2, (y // 2) * 2 + k] for t in slabs]).astype(BF)


def sum_y_kernel(place_ref, p0, p1, p2, p3, keep_ref, send_ref):
    core = place_ref[0]
    for dst, k in ((keep_ref, core), (send_ref, 1 - core)):
        for side in range(2):
            dst[side] = added([t[k, side] for t in (p0, p1, p2, p3)])


def finish_kernel(place_ref, keep_ref, recv_ref, right_ref, gain_ref, gr_ref, gl_ref, gg_ref):
    core = place_ref[0]
    for src, q in ((keep_ref, core), (recv_ref, 1 - core)):
        pick = (iota2(1) == column_source(iota2(0), q)).astype(F32)
        raw = mm_exact(src[0], pick)
        diag = jnp.where(iota2(0) == iota2(1), gain_ref[q].astype(F32), 0.0)
        gr_ref[q] = mm_exact(diag, raw)
        gg_ref[q] = mm_exact(jnp.ones((8, BS), F32), raw * right_ref[q].astype(F32), ((1,), (1,)))[0:1]
        pick = (iota2(0) == row_source(iota2(1), q)).astype(F32)
        gl_ref[q] = mm_exact(pick, src[1])


WHOLE = pl.BlockSpec(memory_space=pltpu.VMEM)
SCALARS = pl.BlockSpec(memory_space=pltpu.SMEM)
ANY = pl.BlockSpec(memory_space=pl.ANY)
TOKENS_SPEC = pl.BlockSpec((2, 64, D // GRID), lambda g, place: (place[1], 0, g))


def kept(*shape, dtype=BF):
    return pltpu.VMEM(shape, dtype)


U_OUT = (kept(HALF, TOK), kept(HALF + STAT, TOK), kept(8, TOK, dtype=F32))
ACT = kept(ROWS, TOK)
STATS = kept(8, TOK, dtype=F32)
SLAB = kept(17, BS, BS)
SCRATCH = (pltpu.VMEM((2, HALF, TOK), F32),)


def call(kernel, place, ins, outs, scratch=(), old=()):
    vmem = [pltpu.with_memory_space_constraint(a, pltpu.VMEM) for a in (*old, *ins)]
    ins = (*vmem[: len(old)], place, *vmem[len(old) :])
    return pl.pallas_call(
        kernel,
        out_shape=outs,
        in_specs=[WHOLE] * len(old) + [SCALARS] + [WHOLE] * (len(ins) - len(old) - 1),
        out_specs=(WHOLE,) * len(outs),
        scratch_shapes=scratch,
        compiler_params=pltpu.CompilerParams(vmem_limit_bytes=VMEM_LIMIT),
    )(*ins)


def swapped(value):
    return lax.ppermute(value, "c", SWAP)


def ring(value, axes, steps):
    return lax.ppermute(value, axes, [(i, (i + steps) % 4) for i in range(4)])


def gathered(value, axes):
    return [value] + [ring(value, axes, s) for s in (1, 2, 3)]


def scattered(slabs, axes):
    return [slabs[0]] + [ring(slabs[s], axes, -s) for s in (1, 2, 3)]


def per_device(inputs, cotangent, right_factor, left_factor, norm_gain):
    core, yh, yl = lax.axis_index("c"), lax.axis_index("yh"), lax.axis_index("yl")
    place = jnp.stack([core, yh, lax.axis_index("x"), lax.axis_index("z"), 2 * yh + yl]).astype(jnp.int32)
    right = right_factor[0]
    left = left_factor[0]
    gain = norm_gain.reshape(2, 1, BS)

    keep, send = call(prep_kernel, place, (right, left, gain), (kept(2, BS, BS),) * 2)
    mine = jnp.stack([keep, swapped(send)])
    stage = kept(2, 4, BS, BS)
    all_right, all_left = call(gather_y_kernel, place, gathered(mine, YS), (stage, stage))
    firsts = call(gather_pair_kernel, place, gathered(all_right, "z") + gathered(all_left, "x"), (SLAB,) * 4)
    rights = [gathered(firsts[0], "x"), gathered(firsts[1], "x")]
    lefts = [gathered(firsts[2], "z"), gathered(firsts[3], "z")]

    x, grad, st = pl.pallas_call(
        tokens_kernel,
        out_shape=(ACT, ACT, STATS),
        grid_spec=pltpu.PrefetchScalarGridSpec(
            num_scalar_prefetch=1, grid=(GRID,), in_specs=[TOKENS_SPEC] * 2, out_specs=(WHOLE,) * 3
        ),
        compiler_params=pltpu.CompilerParams(vmem_limit_bytes=VMEM_LIMIT),
    )(place, inputs, cotangent)

    uo, us, st = call(functools.partial(start_kernel, 0), place, (x, st, *rights[0]), U_OUT, SCRATCH)
    xs, slopes, perms, rmss = [x], [], [], []
    for layer in range(3):
        above = layer + 1
        xn, slope, perm, rms, uo, us, st = call(
            functools.partial(forward_kernel, (layer % 2, above % 2)), place,
            (uo, swapped(us), st, xs[-1], *lefts[layer // 2], *rights[above // 2]),
            (ACT, ACT, ACT, STATS) + U_OUT, SCRATCH,
        )
        xs.append(xn)
        slopes.append(slope)
        perms.append(perm)
        rmss.append(rms)
    rms, *rest = call(
        functools.partial(turn_kernel, 1), place, (uo, swapped(us), st, grad, *lefts[1]), (STATS,) + (SLAB,) * 4 + U_OUT, SCRATCH
    )
    rmss.append(rms)
    grad_lefts = [None, rest[:4]]
    grad_rights = [None, None]
    uo, us, st = rest[4:]
    for layer in (3, 2, 1):
        below = layer - 1
        ins = (
            uo, swapped(us), st, rmss[layer], rmss[below], xs[layer], grad, slopes[below], perms[below],
            *rights[layer // 2], *lefts[below // 2],
        )
        old_right, old_left = grad_rights[layer // 2], grad_lefts[below // 2]
        old, aliases = [], {}
        for slabs, first in ((old_right, 1), (old_left, 5)):
            for k, slab in enumerate(slabs or ()):
                aliases[len(old)] = first + k
                old.append(slab)
        outs = call_into(
            functools.partial(backward_kernel, (layer % 2, below % 2), len(old)), place, ins,
            (ACT,) + (SLAB,) * 8 + U_OUT, SCRATCH, old, aliases,
        )
        grad = outs[0]
        grad_rights[layer // 2] = outs[1:5]
        grad_lefts[below // 2] = outs[5:9]
        uo, us, st = outs[9:]
    summed = kept(16, BS, BS)
    (left_sum,) = call(sum_slab_kernel, place, scattered(grad_lefts[1], "z"), (summed,))
    uo, left_sum = lax.optimization_barrier((uo, left_sum))
    slabs = call_into(
        functools.partial(last_kernel, 0), place, (uo, swapped(us), xs[0]), (SLAB,) * 4, (), grad_rights[0], {k: k for k in range(4)}
    )
    (right_sum,) = call(sum_slab_kernel, place, scattered(grad_rights[1], "x"), (summed,))
    parts = [*scattered(slabs, "x"), right_sum, *scattered(grad_lefts[0], "z"), left_sum]
    outs = call(sum_pair_kernel, place, parts, (stage,) * 8)
    parts = scattered(outs[:4], "z") + scattered(outs[4:], "x")
    outs = call(sum_ring_kernel, place, parts, (kept(2, 2, BS, BS),) * 4)
    sums = kept(2, BS, BS, dtype=F32)
    keep, send = call(sum_y_kernel, place, scattered(outs, YS), (sums, sums))
    whole = jax.ShapeDtypeStruct((2, BS, BS), F32)
    grad_right, grad_left, grad_gain = call(
        finish_kernel, place, (keep, swapped(send), right, gain), (whole, whole, jax.ShapeDtypeStruct((2, 1, BS), F32))
    )
    return grad_right[None], grad_left[None], grad_gain.reshape(1, 2 * BS)


def call_into(kernel, place, ins, outs, scratch, old, aliases):
    vmem = [pltpu.with_memory_space_constraint(a, pltpu.VMEM) for a in (*old, *ins)]
    operands = (*vmem[: len(old)], place, *vmem[len(old) :])
    return pl.pallas_call(
        kernel,
        out_shape=outs,
        in_specs=[WHOLE] * len(old) + [SCALARS] + [WHOLE] * len(ins),
        out_specs=(WHOLE,) * len(outs),
        scratch_shapes=scratch,
        input_output_aliases=aliases,
        compiler_params=pltpu.CompilerParams(vmem_limit_bytes=VMEM_LIMIT),
    )(*operands)


def solution(mesh):
    parts = Mesh(mesh.devices.reshape(2, 2, 4, 4, 2), ("yh", "c", "x", "z", "yl"))
    pipe, fsdp = ("yh", "c"), ("x", "z", "yl")
    return jax.shard_map(
        per_device,
        mesh=parts,
        in_specs=(P(None, fsdp, None), P(None, fsdp, None), P(pipe, fsdp, None, None), P(pipe, fsdp, None, None), P(pipe, fsdp)),
        out_specs=(P(pipe, fsdp, None, None), P(pipe, fsdp, None, None), P(pipe, fsdp)),
        check_vma=False,
    )
```

```python
import functools

import jax
import jax.numpy as jnp
from jax import lax
from jax.experimental import pallas as pl
from jax.experimental.pallas import tpu as pltpu
from jax.sharding import Mesh, PartitionSpec as P

EPSILON = 1e-05
TANH_SLOPE = 0.7978845608028654
CUBIC_TERM = 0.044715

BF = jnp.bfloat16
F32 = jnp.float32
HI = lax.Precision.HIGHEST
SWAP = ((0, 1), (1, 0))
YS = ("yh", "yl")
VMEM_LIMIT = 24 * 1024 * 1024

NB = 64
BS = 128
D = NB * BS
HB = NB // 2
ROWS = HB * BS
HALF = ROWS // 2
TOK = 128
STAT = 16
GRID = 4
BPC = HB // GRID


def mm(a, b):
    return lax.dot_general(a, b, (((1,), (0,)), ((), ())), preferred_element_type=F32)


def mm_ta(a, b):
    return lax.dot_general(a, b, (((0,), (0,)), ((), ())), preferred_element_type=F32)


def mm_tb(a, b):
    return lax.dot_general(a, b, (((1,), (1,)), ((), ())), preferred_element_type=F32)


def mm_exact(a, b, dims=((1,), (0,))):
    return lax.dot_general(a, b, (dims, ((), ())), precision=HI, preferred_element_type=F32)


def iota2(dim):
    return lax.broadcasted_iota(jnp.int32, (BS, BS), dim)


def column_source(dp, q):
    rel = dp // 64
    return ((dp // 32) % 2) * 64 + 2 * (dp % 32) + (rel + q - 2 * rel * q)


def row_source(cp, q):
    rel = cp // 64
    return 4 * ((cp % 64) // 2) + 2 * (rel + q - 2 * rel * q) + cp % 2


def stat_rows(value):
    hi = value.astype(BF)
    rest = value - hi.astype(F32)
    mid = rest.astype(BF)
    lo = (rest - mid.astype(F32)).astype(BF)
    row = lax.broadcasted_iota(jnp.int32, (STAT, TOK), 0)
    out = jnp.where(row == 0, hi.astype(F32), jnp.where(row == 1, mid.astype(F32), lo.astype(F32)))
    return jnp.where(row < 3, out, 0.0).astype(BF)


def stat_total(own_ref, recv_ref):
    rows = recv_ref[pl.ds(HALF, STAT), :].astype(F32)
    return own_ref[0:1, :] + jnp.sum(rows, axis=0, keepdims=True)


def folded(value):
    return jnp.sum(value.reshape(BS // 8, 8, TOK), axis=0)


def back(index, steps):
    return (index + (4 - steps)) % 4


def blocks(place_ref):
    for sx in range(4):
        xm = back(place_ref[2], sx)
        for sz in range(4):
            zm = back(place_ref[3], sz)
            for ym in range(2):
                yield sx, sz, xm, zm, ym, xm * 8 + zm * 2 + ym


def slot(at, yl, k):
    return at * 4 + yl * 2 + k


def rows_of(m):
    return pl.ds(pl.multiple_of(m * BS, BS), BS)


def prep_kernel(place_ref, right_ref, left_ref, gain_ref, keep_ref, send_ref):
    core = place_ref[0]
    for dst, q in ((keep_ref, core), (send_ref, 1 - core)):
        gain_row = gain_ref[q].astype(F32)
        diag = jnp.where(iota2(0) == iota2(1), gain_row, 0.0).astype(BF)
        scaled = mm(diag, right_ref[q]).astype(BF)
        pick = (iota2(0) == column_source(iota2(1), q)).astype(F32).astype(BF)
        dst[0] = mm(scaled, pick).astype(BF)
        pick = (iota2(1) == row_source(iota2(0), q)).astype(F32).astype(BF)
        dst[1] = mm(pick, left_ref[q]).astype(BF)


def taken(pieces, s, k, size, at):
    if s == 2:
        return pieces[2 + k // 2][(k // 2) * (size // 8) + (k % 2) * size + at]
    return pieces[s + s // 3][k * size + at]


def gather_y_kernel(place_ref, p0, p1, p2, p3, right_ref, left_ref):
    core = place_ref[0]
    for s, piece in enumerate((p0, p1, p2, p3)):
        y = back(place_ref[4], s)
        for k in range(2):
            layer = (y // 2) * 2 + (core + k) % 2
            right_ref[layer * 2 + y % 2] = piece[k, 0]
            left_ref[layer * 2 + y % 2] = piece[k, 1]


def gather_pair_kernel(place_ref, *refs):
    for pieces, index, out in ((refs[:5], 3, refs[10]), (refs[5:10], 2, refs[11])):
        for s in range(4):
            at = back(place_ref[index], s)
            for k in range(4):
                for yl in range(2):
                    out[k * 8 + at * 2 + yl] = taken(pieces, s, k, 2, yl)


def tokens_kernel(place_ref, in_ref, cot_ref, x_ref, grad_ref, stat_ref):
    core = place_ref[0]
    base = pl.program_id(0) * BPC
    total = jnp.zeros((8, TOK), F32)
    for i in range(BPC):
        lanes = pl.ds(pl.multiple_of((2 * i + core) * BS, BS), BS)
        x = in_ref[:, :, lanes].reshape(TOK, BS).astype(F32).T
        x_ref[rows_of(base + i), :] = x.astype(BF)
        total = total + folded(x * x)
        grad_ref[rows_of(base + i), :] = cot_ref[:, :, lanes].reshape(TOK, BS).astype(F32).T.astype(BF)
    total = jnp.broadcast_to(jnp.sum(total, axis=0, keepdims=True), (8, TOK))

    @pl.when(pl.program_id(0) == 0)
    def _():
        stat_ref[...] = jnp.zeros_like(stat_ref)

    stat_ref[...] += total


def put_forward(scr, m, product):
    for part in range(2):
        for h in range(2):
            scr[part, pl.ds(m * 2 + h, 32, stride=64), :] = product[part * 64 + h * 32 :][:32]


def put_backward(scr, m, product):
    for part in range(2):
        scr[part, pl.ds(m, 64, stride=32), :] = product[part * 64 :][:64]


def flush(scr, total, own_ref, send_ref, stat_ref):
    own_ref[...] = scr[0].astype(BF)
    send_ref[pl.ds(0, HALF), :] = scr[1].astype(BF)
    send_ref[pl.ds(HALF, STAT), :] = stat_rows(total)
    stat_ref[...] = jnp.broadcast_to(total, stat_ref.shape)


def gelu_parts(v):
    sq = v * v
    t = jnp.tanh(v * (TANH_SLOPE + (TANH_SLOPE * CUBIC_TERM) * sq))
    half = 0.5 * t + 0.5
    slope = half + (v * (1.0 - t * t)) * (0.5 * TANH_SLOPE + (1.5 * TANH_SLOPE * CUBIC_TERM) * sq)
    return v * half, slope


def rms_of(own_stat, recv_ref):
    return lax.rsqrt(stat_total(own_stat, recv_ref) * (1.0 / D) + EPSILON)


def permuted_block(own_ref, recv_ref, m, rms):
    rows = pl.ds(pl.multiple_of(m * 64, 64), 64)
    both = jnp.concatenate([own_ref[rows, :], recv_ref[rows, :]], axis=0)
    if rms is None:
        return both
    return (both.astype(F32) * rms).astype(BF)


def start_kernel(place_ref, x_ref, st_ref, w0, w1, w2, w3, w4, own_ref, send_ref, stat_ref, scr):
    rights = (w0, w1, w2, w3, w4)
    for sx, sz, xm, zm, ym, m in blocks(place_ref):
        put_forward(scr, m, mm_ta(taken(rights, sx, 0, 8, zm * 2 + ym), x_ref[rows_of(m), :]))
    flush(scr, st_ref[0:1, :], own_ref, send_ref, stat_ref)


def forward_kernel(
    layer, place_ref, uo_ref, ur_ref, us_ref, x_ref, l0, l1, l2, l3, l4, w0, w1, w2, w3, w4,
    xn_ref, slope_ref, perm_ref, rms_ref, own_ref, send_ref, stat_ref, scr,
):
    lefts, rights = (l0, l1, l2, l3, l4), (w0, w1, w2, w3, w4)
    rms = rms_of(us_ref, ur_ref)
    rms_ref[...] = jnp.broadcast_to(rms, rms_ref.shape)
    total = jnp.zeros((8, TOK), F32)
    for sx, sz, xm, zm, ym, m in blocks(place_ref):
        rows = rows_of(m)
        perm = permuted_block(uo_ref, ur_ref, m, rms)
        perm_ref[rows, :] = perm
        value, slope = gelu_parts(mm_ta(taken(lefts, sz, layer, 8, xm * 2 + ym), perm))
        slope_ref[rows, :] = slope.astype(BF)
        xb = (x_ref[rows, :].astype(F32) + value).astype(BF)
        xn_ref[rows, :] = xb
        x = xb.astype(F32)
        total = total + folded(x * x)
        put_forward(scr, m, mm_ta(taken(rights, sx, layer + 1, 8, zm * 2 + ym), xb))
    flush(scr, jnp.sum(total, axis=0, keepdims=True), own_ref, send_ref, stat_ref)


def left_backward(grad, slope, perm, left, rms, m, scr):
    grad_pre = (grad.astype(F32) * slope).astype(BF)
    grad_left = mm_tb(perm, grad_pre).astype(BF)
    grad_perm = mm(left, grad_pre)
    put_backward(scr, m, grad_perm * rms)
    return grad_left, folded(grad_perm * perm.astype(F32))


def turn_kernel(
    layer, place_ref, uo_ref, ur_ref, us_ref, grad_ref, l0, l1, l2, l3, l4,
    rms_ref, g0, g1, g2, g3, own_ref, send_ref, stat_ref, scr,
):
    lefts, outs = (l0, l1, l2, l3, l4), (g0, g1, g2, g3)
    rms = rms_of(us_ref, ur_ref)
    rms_ref[...] = jnp.broadcast_to(rms, rms_ref.shape)
    total = jnp.zeros((8, TOK), F32)
    for sx, sz, xm, zm, ym, m in blocks(place_ref):
        perm = permuted_block(uo_ref, ur_ref, m, rms)
        left = taken(lefts, sz, layer, 8, xm * 2 + ym)
        slope = gelu_parts(mm_ta(left, perm))[1]
        outs[sz][slot(xm, ym, layer % 2)], add = left_backward(grad_ref[rows_of(m), :], slope, perm, left, rms, m, scr)
        total = total + add
    flush(scr, jnp.sum(total, axis=0, keepdims=True), own_ref, send_ref, stat_ref)


def backward_kernel(layer, n_old, *refs):
    refs = refs[n_old:]
    place_ref, go_ref, gr_ref, gs_ref, rms_ref, rms_below_ref, x_ref, grad_ref, slope_ref, perm_ref = refs[:10]
    rights, lefts, refs = refs[10:15], refs[15:20], refs[20:]
    out_right, out_left = refs[:4], refs[4:8]
    own_ref, send_ref, stat_ref = refs[8:11]
    new_ref, scr = refs[11] if layer > 1 else None, refs[-1]
    below = layer - 1
    rms = rms_ref[0:1, :]
    rms_below = rms_below_ref[0:1, :]
    coef = stat_total(gs_ref, gr_ref) * (rms * rms * (1.0 / D))
    total = jnp.zeros((8, TOK), F32)
    for sx, sz, xm, zm, ym, m in blocks(place_ref):
        rows = rows_of(m)
        gf = permuted_block(go_ref, gr_ref, m, None)
        x = x_ref[rows, :]
        out_right[sx][slot(zm, ym, layer % 2)] = mm_tb(x, gf).astype(BF)
        grad = grad_ref[rows, :].astype(F32) + mm(taken(rights, sx, layer, 8, zm * 2 + ym), gf) - x.astype(F32) * coef
        grad = grad.astype(BF)
        if new_ref is not None:
            new_ref[rows, :] = grad
        out_left[sz][slot(xm, ym, below % 2)], add = left_backward(
            grad, slope_ref[rows, :].astype(F32), perm_ref[rows, :], taken(lefts, sz, below, 8, xm * 2 + ym), rms_below, m, scr
        )
        total = total + add
    flush(scr, jnp.sum(total, axis=0, keepdims=True), own_ref, send_ref, stat_ref)


def last_kernel(k, b0, b1, b2, b3, place_ref, go_ref, gr_ref, x_ref, o0, o1, o2, o3):
    del b0, b1, b2, b3
    outs = (o0, o1, o2, o3)
    for sx, sz, xm, zm, ym, m in blocks(place_ref):
        gf = permuted_block(go_ref, gr_ref, m, None)
        outs[sx][slot(zm, ym, k)] = mm_tb(x_ref[rows_of(m), :], gf).astype(BF)


def added(parts):
    a, b, c, d = (p.astype(F32) for p in parts)
    return (a + b) + (c + d)


def sum_slab_kernel(place_ref, a_ref, b_ref, c_ref, d_ref, out_ref):
    del place_ref
    for i in range(16):
        out_ref[i] = added((a_ref[i], b_ref[i], c_ref[i], d_ref[i])).astype(BF)


def sum_pair_kernel(place_ref, *refs):
    sources, outs = refs[:10], refs[10:]
    for side, index in ((0, 3), (1, 2)):
        slabs, ready = sources[side * 5 :][:4], sources[side * 5 + 4]
        for s in range(4):
            at = back(place_ref[index], s)
            for yl in range(2):
                for k in range(2):
                    outs[side * 4 + s][yl, k] = added([t[slot(at, yl, k)] for t in slabs]).astype(BF)
                    outs[side * 4 + s][yl, 2 + k] = ready[slot(at, yl, k)]


def sum_ring_kernel(place_ref, *refs):
    sources, outs = refs[:8], refs[8:]
    for side in range(2):
        slabs = sources[side * 4 :][:4]
        for s in range(4):
            y = back(place_ref[4], s)
            for k in range(2):
                outs[s][k, side] = added([t[y % 2, (y // 2) * 2 + k] for t in slabs]).astype(BF)


def sum_y_kernel(place_ref, p0, p1, p2, p3, keep_ref, send_ref):
    core = place_ref[0]
    for dst, k in ((keep_ref, core), (send_ref, 1 - core)):
        for side in range(2):
            dst[side] = added([t[k, side] for t in (p0, p1, p2, p3)])


def finish_kernel(place_ref, keep_ref, recv_ref, right_ref, gain_ref, gr_ref, gl_ref, gg_ref):
    core = place_ref[0]
    for src, q in ((keep_ref, core), (recv_ref, 1 - core)):
        pick = (iota2(1) == column_source(iota2(0), q)).astype(F32)
        raw = mm_exact(src[0], pick)
        diag = jnp.where(iota2(0) == iota2(1), gain_ref[q].astype(F32), 0.0)
        gr_ref[q] = mm_exact(diag, raw)
        gg_ref[q] = mm_exact(jnp.ones((8, BS), F32), raw * right_ref[q].astype(F32), ((1,), (1,)))[0:1]
        pick = (iota2(0) == row_source(iota2(1), q)).astype(F32)
        gl_ref[q] = mm_exact(pick, src[1])


WHOLE = pl.BlockSpec(memory_space=pltpu.VMEM)
SCALARS = pl.BlockSpec(memory_space=pltpu.SMEM)
ANY = pl.BlockSpec(memory_space=pl.ANY)
TOKENS_SPEC = pl.BlockSpec((2, 64, D // GRID), lambda g, place: (place[1], 0, g))


def kept(*shape, dtype=BF):
    return pltpu.VMEM(shape, dtype)


U_OUT = (kept(HALF, TOK), kept(HALF + STAT, TOK), kept(8, TOK, dtype=F32))
ACT = kept(ROWS, TOK)
STATS = kept(8, TOK, dtype=F32)
SLAB = kept(17, BS, BS)
SCRATCH = (pltpu.VMEM((2, HALF, TOK), F32),)


def call(kernel, place, ins, outs, scratch=(), old=()):
    vmem = [pltpu.with_memory_space_constraint(a, pltpu.VMEM) for a in (*old, *ins)]
    ins = (*vmem[: len(old)], place, *vmem[len(old) :])
    return pl.pallas_call(
        kernel,
        out_shape=outs,
        in_specs=[WHOLE] * len(old) + [SCALARS] + [WHOLE] * (len(ins) - len(old) - 1),
        out_specs=(WHOLE,) * len(outs),
        scratch_shapes=scratch,
        compiler_params=pltpu.CompilerParams(vmem_limit_bytes=VMEM_LIMIT),
    )(*ins)


def swapped(value):
    return lax.ppermute(value, "c", SWAP)


def ring(value, axes, steps):
    return lax.ppermute(value, axes, [(i, (i + steps) % 4) for i in range(4)])


def gathered(value, axes):
    return [value] + [ring(value, axes, s) for s in (1, 2, 3)]


def ring_gathered(value, axes):
    half = value.shape[0] // 2
    up, down = ring(value, axes, 1), ring(value, axes, -1)
    spare = half // 16
    return [value, up, ring(up[: half + spare], axes, 1), ring(down[half - spare :], axes, -1), down]


def scattered(slabs, axes):
    return [slabs[0]] + [ring(slabs[s], axes, -s) for s in (1, 2, 3)]


def per_device(inputs, cotangent, right_factor, left_factor, norm_gain):
    core, yh, yl = lax.axis_index("c"), lax.axis_index("yh"), lax.axis_index("yl")
    place = jnp.stack([core, yh, lax.axis_index("x"), lax.axis_index("z"), 2 * yh + yl]).astype(jnp.int32)
    right = right_factor[0]
    left = left_factor[0]
    gain = norm_gain.reshape(2, 1, BS)

    keep, send = call(prep_kernel, place, (right, left, gain), (kept(2, BS, BS),) * 2)
    mine = jnp.stack([keep, swapped(send)])
    stage = kept(2, 4, BS, BS)
    part = kept(8, BS, BS)
    all_right, all_left = call(gather_y_kernel, place, gathered(mine, YS), (part, part))
    firsts = call(
        gather_pair_kernel, place, ring_gathered(all_right, "z") + ring_gathered(all_left, "x"), (kept(32, BS, BS),) * 2
    )
    rights, lefts = ring_gathered(firsts[0], "x"), ring_gathered(firsts[1], "z")

    x, grad, st = pl.pallas_call(
        tokens_kernel,
        out_shape=(ACT, ACT, STATS),
        grid_spec=pltpu.PrefetchScalarGridSpec(
            num_scalar_prefetch=1, grid=(GRID,), in_specs=[TOKENS_SPEC] * 2, out_specs=(WHOLE,) * 3
        ),
        compiler_params=pltpu.CompilerParams(vmem_limit_bytes=VMEM_LIMIT),
    )(place, inputs, cotangent)

    uo, us, st = call(start_kernel, place, (x, st, *rights), U_OUT, SCRATCH)
    xs, slopes, perms, rmss = [x], [], [], []
    for layer in range(3):
        xn, slope, perm, rms, uo, us, st = call(
            functools.partial(forward_kernel, layer), place,
            (uo, swapped(us), st, xs[-1], *lefts, *rights),
            (ACT, ACT, ACT, STATS) + U_OUT, SCRATCH,
        )
        xs.append(xn)
        slopes.append(slope)
        perms.append(perm)
        rmss.append(rms)
    rms, *rest = call(
        functools.partial(turn_kernel, 3), place, (uo, swapped(us), st, grad, *lefts), (STATS,) + (SLAB,) * 4 + U_OUT, SCRATCH
    )
    rmss.append(rms)
    grad_lefts = [None, rest[:4]]
    grad_rights = [None, None]
    uo, us, st = rest[4:]
    for layer in (3, 2, 1):
        below = layer - 1
        ins = (
            uo, swapped(us), st, rmss[layer], rmss[below], xs[layer], grad, slopes[below], perms[below],
            *rights, *lefts,
        )
        old_right, old_left = grad_rights[layer // 2], grad_lefts[below // 2]
        old, aliases = [], {}
        for slabs, first in ((old_right, 0), (old_left, 4)):
            for k, slab in enumerate(slabs or ()):
                aliases[len(old)] = first + k
                old.append(slab)
        outs = call_into(
            functools.partial(backward_kernel, layer, len(old)), place, ins,
            (SLAB,) * 8 + U_OUT + (ACT,) * (layer > 1), SCRATCH, old, aliases,
        )
        grad_rights[layer // 2] = outs[:4]
        grad_lefts[below // 2] = outs[4:8]
        uo, us, st, *grad = outs[8:]
        grad = grad[0] if grad else None
    summed = kept(16, BS, BS)
    (left_sum,) = call(sum_slab_kernel, place, scattered(grad_lefts[1], "z"), (summed,))
    uo, left_sum = lax.optimization_barrier((uo, left_sum))
    slabs = call_into(
        functools.partial(last_kernel, 0), place, (uo, swapped(us), xs[0]), (SLAB,) * 4, (), grad_rights[0], {k: k for k in range(4)}
    )
    (right_sum,) = call(sum_slab_kernel, place, scattered(grad_rights[1], "x"), (summed,))
    parts = [*scattered(slabs, "x"), right_sum, *scattered(grad_lefts[0], "z"), left_sum]
    outs = call(sum_pair_kernel, place, parts, (stage,) * 8)
    parts = scattered(outs[:4], "z") + scattered(outs[4:], "x")
    outs = call(sum_ring_kernel, place, parts, (kept(2, 2, BS, BS),) * 4)
    sums = kept(2, BS, BS, dtype=F32)
    keep, send = call(sum_y_kernel, place, scattered(outs, YS), (sums, sums))
    whole = jax.ShapeDtypeStruct((2, BS, BS), F32)
    grad_right, grad_left, grad_gain = call(
        finish_kernel, place, (keep, swapped(send), right, gain), (whole, whole, jax.ShapeDtypeStruct((2, 1, BS), F32))
    )
    return grad_right[None], grad_left[None], grad_gain.reshape(1, 2 * BS)


def call_into(kernel, place, ins, outs, scratch, old, aliases):
    vmem = [pltpu.with_memory_space_constraint(a, pltpu.VMEM) for a in (*old, *ins)]
    operands = (*vmem[: len(old)], place, *vmem[len(old) :])
    return pl.pallas_call(
        kernel,
        out_shape=outs,
        in_specs=[WHOLE] * len(old) + [SCALARS] + [WHOLE] * len(ins),
        out_specs=(WHOLE,) * len(outs),
        scratch_shapes=scratch,
        input_output_aliases=aliases,
        compiler_params=pltpu.CompilerParams(vmem_limit_bytes=VMEM_LIMIT),
    )(*operands)


def solution(mesh):
    parts = Mesh(mesh.devices.reshape(2, 2, 4, 4, 2), ("yh", "c", "x", "z", "yl"))
    pipe, fsdp = ("yh", "c"), ("x", "z", "yl")
    return jax.shard_map(
        per_device,
        mesh=parts,
        in_specs=(P(None, fsdp, None), P(None, fsdp, None), P(pipe, fsdp, None, None), P(pipe, fsdp, None, None), P(pipe, fsdp)),
        out_specs=(P(pipe, fsdp, None, None), P(pipe, fsdp, None, None), P(pipe, fsdp)),
        check_vma=False,
    )
```

```python
import functools

import jax
import jax.numpy as jnp
from jax import lax
from jax.experimental import pallas as pl
from jax.experimental.pallas import tpu as pltpu
from jax.sharding import Mesh, PartitionSpec as P

EPSILON = 1e-05
TANH_SLOPE = 0.7978845608028654
CUBIC_TERM = 0.044715

BF = jnp.bfloat16
F32 = jnp.float32
HI = lax.Precision.HIGHEST
SWAP = ((0, 1), (1, 0))
YS = ("yh", "yl")
VMEM_LIMIT = 24 * 1024 * 1024

NB = 64
BS = 128
D = NB * BS
HB = NB // 2
ROWS = HB * BS
HALF = ROWS // 2
TOK = 128
STAT = 16
FORWARD = (65, 64)
BACKWARD = (33, 32)
GRID = 4
BPC = HB // GRID


def mm(a, b):
    return lax.dot_general(a, b, (((1,), (0,)), ((), ())), preferred_element_type=F32)


def mm_ta(a, b):
    return mm(a.T, b)


def mm_tb(a, b):
    return mm(a, b.T)


def mm_exact(a, b, dims=((1,), (0,))):
    return lax.dot_general(a, b, (dims, ((), ())), precision=HI, preferred_element_type=F32)


def iota2(dim):
    return lax.broadcasted_iota(jnp.int32, (BS, BS), dim)


def column_source(dp, q):
    rel = dp // 64
    return ((dp // 32) % 2) * 64 + 2 * (dp % 32) + (rel + q - 2 * rel * q)


def row_source(cp, q):
    rel = cp // 64
    return 4 * ((cp % 64) // 2) + 2 * (rel + q - 2 * rel * q) + cp % 2


def stat_rows(value):
    hi = value.astype(BF)
    rest = value - hi.astype(F32)
    mid = rest.astype(BF)
    lo = (rest - mid.astype(F32)).astype(BF)
    row = lax.broadcasted_iota(jnp.int32, (STAT, TOK), 0)
    out = jnp.where(row == 0, hi.astype(F32), jnp.where(row == 1, mid.astype(F32), lo.astype(F32)))
    return jnp.where(row < 3, out, 0.0).astype(BF)


def stat_total(own_ref, recv_ref):
    rows = recv_ref[pl.ds(HALF, STAT), :].astype(F32)
    return own_ref[0:1, :] + jnp.sum(rows, axis=0, keepdims=True)


def folded(value):
    return jnp.sum(value.reshape(BS // 8, 8, TOK), axis=0)


def back(index, steps):
    return (index + (4 - steps)) % 4


def blocks(place_ref):
    for sx in range(4):
        xm = back(place_ref[2], sx)
        for sz in range(4):
            zm = back(place_ref[3], sz)
            for ym in range(2):
                yield sx, sz, xm, zm, ym, xm * 8 + zm * 2 + ym


def slot(layer, at, yl):
    return layer * 8 + at * 2 + yl


def rows_of(m):
    return pl.ds(pl.multiple_of(m * BS, BS), BS)


def prep_kernel(place_ref, right_ref, left_ref, gain_ref, keep_ref, send_ref):
    core = place_ref[0]
    for dst, q in ((keep_ref, core), (send_ref, 1 - core)):
        gain_row = gain_ref[q].astype(F32)
        diag = jnp.where(iota2(0) == iota2(1), gain_row, 0.0).astype(BF)
        scaled = mm(diag, right_ref[q]).astype(BF)
        pick = (iota2(0) == column_source(iota2(1), q)).astype(F32).astype(BF)
        dst[0] = mm(scaled, pick).astype(BF)
        pick = (iota2(1) == row_source(iota2(0), q)).astype(F32).astype(BF)
        dst[1] = mm(pick, left_ref[q]).astype(BF)


def taken(pieces, s, k, size, at):
    if s == 2:
        return pieces[2 + k // 2][(k // 2) * (size // 8) + (k % 2) * size + at]
    return pieces[s + s // 3][k * size + at]


def gather_y_kernel(place_ref, p0, p1, p2, p3, right_ref, left_ref):
    core = place_ref[0]
    for s, piece in enumerate((p0, p1, p2, p3)):
        y = back(place_ref[4], s)
        for k in range(2):
            layer = (y // 2) * 2 + (core + k) % 2
            right_ref[layer * 2 + y % 2] = piece[k, 0]
            left_ref[layer * 2 + y % 2] = piece[k, 1]


def gather_pair_kernel(place_ref, *refs):
    for pieces, index, out in ((refs[:5], 3, refs[10]), (refs[5:10], 2, refs[11])):
        for s in range(4):
            at = back(place_ref[index], s)
            for k in range(4):
                for yl in range(2):
                    out[k * 8 + at * 2 + yl] = taken(pieces, s, k, 2, yl)


def tokens_kernel(place_ref, in_ref, cot_ref, x_ref, grad_ref, stat_ref):
    core = place_ref[0]
    base = pl.program_id(0) * BPC
    total = jnp.zeros((8, TOK), F32)
    for i in range(BPC):
        lanes = pl.ds(pl.multiple_of((2 * i + core) * BS, BS), BS)
        x = in_ref[:, :, lanes].reshape(TOK, BS).astype(F32).T
        x_ref[rows_of(base + i), :] = x.astype(BF)
        total = total + folded(x * x)
        grad_ref[rows_of(base + i), :] = cot_ref[:, :, lanes].reshape(TOK, BS).astype(F32).T.astype(BF)
    total = jnp.broadcast_to(jnp.sum(total, axis=0, keepdims=True), (8, TOK))

    @pl.when(pl.program_id(0) == 0)
    def _():
        stat_ref[...] = jnp.zeros_like(stat_ref)

    stat_ref[...] += total


def put_forward(scr, m, product):
    for part in range(2):
        for h in range(2):
            scr[part, pl.ds(m * 2 + h, 32, stride=FORWARD[0]), :] = product[part * 64 + h * 32 :][:32]


def put_backward(scr, m, product):
    for part in range(2):
        scr[part, pl.ds(m, 64, stride=BACKWARD[0]), :] = product[part * 64 :][:64]


def flush(runs, scr, total, own_ref, send_ref, stat_ref):
    pitch, used = runs
    for i in range(HALF // used):
        own_ref[pl.ds(i * used, used), :] = scr[0, pl.ds(i * pitch, used), :].astype(BF)
        send_ref[pl.ds(i * used, used), :] = scr[1, pl.ds(i * pitch, used), :].astype(BF)
    send_ref[pl.ds(HALF, STAT), :] = stat_rows(total)
    stat_ref[...] = jnp.broadcast_to(total, stat_ref.shape)


def gelu_parts(v):
    sq = v * v
    t = jnp.tanh(v * (TANH_SLOPE + (TANH_SLOPE * CUBIC_TERM) * sq))
    half = 0.5 * t + 0.5
    slope = half + (v * (1.0 - t * t)) * (0.5 * TANH_SLOPE + (1.5 * TANH_SLOPE * CUBIC_TERM) * sq)
    return v * half, slope


def rms_of(own_stat, recv_ref):
    return lax.rsqrt(stat_total(own_stat, recv_ref) * (1.0 / D) + EPSILON)


def permuted_block(own_ref, recv_ref, m, rms):
    rows = pl.ds(pl.multiple_of(m * 64, 64), 64)
    both = jnp.concatenate([own_ref[rows, :], recv_ref[rows, :]], axis=0)
    if rms is None:
        return both
    return (both.astype(F32) * rms).astype(BF)


def start_kernel(place_ref, x_ref, st_ref, w0, w1, w2, w3, w4, own_ref, send_ref, stat_ref, scr):
    rights = (w0, w1, w2, w3, w4)
    for sx, sz, xm, zm, ym, m in blocks(place_ref):
        put_forward(scr, m, mm_ta(taken(rights, sx, 0, 8, zm * 2 + ym), x_ref[rows_of(m), :]))
    flush(FORWARD, scr, st_ref[0:1, :], own_ref, send_ref, stat_ref)


def forward_kernel(
    layer, place_ref, uo_ref, ur_ref, us_ref, x_ref, l0, l1, l2, l3, l4, w0, w1, w2, w3, w4,
    xn_ref, slope_ref, perm_ref, rms_ref, own_ref, send_ref, stat_ref, scr,
):
    lefts, rights = (l0, l1, l2, l3, l4), (w0, w1, w2, w3, w4)
    rms = rms_of(us_ref, ur_ref)
    rms_ref[...] = jnp.broadcast_to(rms, rms_ref.shape)
    total = jnp.zeros((8, TOK), F32)
    for sx, sz, xm, zm, ym, m in blocks(place_ref):
        rows = rows_of(m)
        perm = permuted_block(uo_ref, ur_ref, m, rms)
        perm_ref[rows, :] = perm
        value, slope = gelu_parts(mm_ta(taken(lefts, sz, layer, 8, xm * 2 + ym), perm))
        slope_ref[rows, :] = slope.astype(BF)
        xb = (x_ref[rows, :].astype(F32) + value).astype(BF)
        xn_ref[rows, :] = xb
        x = xb.astype(F32)
        total = total + folded(x * x)
        put_forward(scr, m, mm_ta(taken(rights, sx, layer + 1, 8, zm * 2 + ym), xb))
    flush(FORWARD, scr, jnp.sum(total, axis=0, keepdims=True), own_ref, send_ref, stat_ref)


def left_chain(grad, slope, perm, left, rms, m, scr):
    grad_pre = (grad.astype(F32) * slope).astype(BF)
    grad_perm = mm(left, grad_pre)
    put_backward(scr, m, grad_perm * rms)
    return grad_pre, folded(grad_perm * perm.astype(F32))


def turn_kernel(
    layer, place_ref, uo_ref, ur_ref, us_ref, grad_ref, l0, l1, l2, l3, l4,
    rms_ref, perm_ref, pre_ref, own_ref, send_ref, stat_ref, scr,
):
    lefts = (l0, l1, l2, l3, l4)
    rms = rms_of(us_ref, ur_ref)
    rms_ref[...] = jnp.broadcast_to(rms, rms_ref.shape)
    total = jnp.zeros((8, TOK), F32)
    for sx, sz, xm, zm, ym, m in blocks(place_ref):
        rows = rows_of(m)
        perm = permuted_block(uo_ref, ur_ref, m, rms)
        perm_ref[rows, :] = perm
        left = taken(lefts, sz, layer, 8, xm * 2 + ym)
        slope = gelu_parts(mm_ta(left, perm))[1]
        pre_ref[rows, :], add = left_chain(grad_ref[rows, :], slope, perm, left, rms, m, scr)
        total = total + add
    flush(BACKWARD, scr, jnp.sum(total, axis=0, keepdims=True), own_ref, send_ref, stat_ref)


def backward_kernel(layer, *refs):
    place_ref, go_ref, gr_ref, gs_ref, rms_ref, rms_below_ref, x_ref, grad_ref, slope_ref, perm_ref = refs[:10]
    rights, lefts, refs = refs[10:15], refs[15:20], refs[20:]
    pre_ref, own_ref, send_ref, stat_ref = refs[:4]
    new_ref, scr = refs[4] if layer > 1 else None, refs[-1]
    below = layer - 1
    rms = rms_ref[0:1, :]
    rms_below = rms_below_ref[0:1, :]
    coef = stat_total(gs_ref, gr_ref) * (rms * rms * (1.0 / D))
    total = jnp.zeros((8, TOK), F32)
    for sx, sz, xm, zm, ym, m in blocks(place_ref):
        rows = rows_of(m)
        gf = permuted_block(go_ref, gr_ref, m, None)
        grad = grad_ref[rows, :].astype(F32) + mm(taken(rights, sx, layer, 8, zm * 2 + ym), gf)
        grad = (grad - x_ref[rows, :].astype(F32) * coef).astype(BF)
        if new_ref is not None:
            new_ref[rows, :] = grad
        left = taken(lefts, sz, below, 8, xm * 2 + ym)
        pre_ref[rows, :], add = left_chain(
            grad, slope_ref[rows, :].astype(F32), perm_ref[rows, :], left, rms_below, m, scr
        )
        total = total + add
    flush(BACKWARD, scr, jnp.sum(total, axis=0, keepdims=True), own_ref, send_ref, stat_ref)


def factor_kernel(right_layer, left_layer, n_old, *refs):
    refs = refs[n_old:]
    place_ref, refs = refs[0], refs[1:]
    if right_layer is not None:
        (go_ref, gr_ref, x_ref), refs = refs[:3], refs[3:]
    if left_layer is not None:
        (perm_ref, pre_ref), refs = refs[:2], refs[2:]
    for sx, sz, xm, zm, ym, m in blocks(place_ref):
        rows = rows_of(m)
        if right_layer is not None:
            gf = permuted_block(go_ref, gr_ref, m, None)
            refs[sx][slot(right_layer, zm, ym)] = mm_tb(x_ref[rows, :], gf).astype(BF)
        if left_layer is not None:
            refs[sz - 4][slot(left_layer, xm, ym)] = mm_tb(perm_ref[rows, :], pre_ref[rows, :]).astype(BF)


def added(parts):
    parts = [p.astype(F32) for p in parts]
    total = parts[0] + parts[1]
    return total + parts[2] if len(parts) == 3 else total + (parts[2] + parts[3]) if len(parts) == 4 else total


def pass_kernel(place_ref, down_ref, up_ref, lo_ref, hi_ref, down_out, up_out):
    del place_ref
    for i in range(16):
        down_out[i] = added((down_ref[i], lo_ref[i])).astype(BF)
        down_out[16 + i] = down_ref[16 + i]
        up_out[i] = up_ref[i]
        up_out[16 + i] = added((up_ref[16 + i], hi_ref[i])).astype(BF)


def sum_pair_kernel(place_ref, *refs):
    sources, outs = refs[:6], refs[6:]
    for side, index in ((0, 3), (1, 2)):
        slabs = sources[side * 3 :][:3]
        for s in range(4):
            at = back(place_ref[index], s)
            for yl in range(2):
                for layer in range(4):
                    outs[side * 4 + s][yl, layer] = added([t[slot(layer, at, yl)] for t in slabs]).astype(BF)


def sum_ring_kernel(place_ref, *refs):
    sources, outs = refs[:8], refs[8:]
    for side in range(2):
        slabs = sources[side * 4 :][:4]
        for s in range(4):
            y = back(place_ref[4], s)
            for k in range(2):
                outs[s][k, side] = added([t[y % 2, (y // 2) * 2 + k] for t in slabs]).astype(BF)


def sum_y_kernel(place_ref, p0, p1, p2, p3, keep_ref, send_ref):
    core = place_ref[0]
    for dst, k in ((keep_ref, core), (send_ref, 1 - core)):
        for side in range(2):
            dst[side] = added([t[k, side] for t in (p0, p1, p2, p3)])


def finish_kernel(place_ref, keep_ref, recv_ref, right_ref, gain_ref, gr_ref, gl_ref, gg_ref):
    core = place_ref[0]
    for src, q in ((keep_ref, core), (recv_ref, 1 - core)):
        pick = (iota2(1) == column_source(iota2(0), q)).astype(F32)
        raw = mm_exact(src[0], pick)
        diag = jnp.where(iota2(0) == iota2(1), gain_ref[q].astype(F32), 0.0)
        gr_ref[q] = mm_exact(diag, raw)
        gg_ref[q] = mm_exact(jnp.ones((8, BS), F32), raw * right_ref[q].astype(F32), ((1,), (1,)))[0:1]
        pick = (iota2(0) == row_source(iota2(1), q)).astype(F32)
        gl_ref[q] = mm_exact(pick, src[1])


WHOLE = pl.BlockSpec(memory_space=pltpu.VMEM)
SCALARS = pl.BlockSpec(memory_space=pltpu.SMEM)
ANY = pl.BlockSpec(memory_space=pl.ANY)
TOKENS_SPEC = pl.BlockSpec((2, 64, D // GRID), lambda g, place: (place[1], 0, g))


def kept(*shape, dtype=BF):
    return pltpu.VMEM(shape, dtype)


U_OUT = (kept(HALF, TOK), kept(HALF + STAT, TOK), kept(8, TOK, dtype=F32))
ACT = kept(ROWS, TOK)
STATS = kept(8, TOK, dtype=F32)
SLAB = kept(32, BS, BS)
SCRATCH = (pltpu.VMEM((2, HALF + 64, TOK), F32),)


def call(kernel, place, ins, outs, scratch=(), old=()):
    vmem = [pltpu.with_memory_space_constraint(a, pltpu.VMEM) for a in (*old, *ins)]
    ins = (*vmem[: len(old)], place, *vmem[len(old) :])
    return pl.pallas_call(
        kernel,
        out_shape=outs,
        in_specs=[WHOLE] * len(old) + [SCALARS] + [WHOLE] * (len(ins) - len(old) - 1),
        out_specs=(WHOLE,) * len(outs),
        scratch_shapes=scratch,
        compiler_params=pltpu.CompilerParams(vmem_limit_bytes=VMEM_LIMIT),
    )(*ins)


def swapped(value):
    return lax.ppermute(value, "c", SWAP)


def ring(value, axes, steps):
    return lax.ppermute(value, axes, [(i, (i + steps) % 4) for i in range(4)])


def gathered(value, axes):
    return [value] + [ring(value, axes, s) for s in (1, 2, 3)]


def ring_gathered(value, axes):
    half = value.shape[0] // 2
    up, down = ring(value, axes, 1), ring(value, axes, -1)
    spare = half // 16
    return [value, up, ring(up[: half + spare], axes, 1), ring(down[half - spare :], axes, -1), down]


def scattered(slabs, axes):
    return [slabs[0]] + [ring(slabs[s], axes, -s) for s in (1, 2, 3)]


def ring_reduced(right_slabs, left_slabs, place):
    sides = ((right_slabs, "x"), (left_slabs, "z"))
    far = [(ring(slabs[2][:16], axes, -1), ring(slabs[2][16:], axes, 1)) for slabs, axes in sides]
    parts = []
    for (slabs, axes), got in zip(sides, far):
        down, up = call(pass_kernel, place, (slabs[1], slabs[3], *got), (SLAB, SLAB))
        parts += [slabs[0], ring(down, axes, -1), ring(up, axes, 1)]
    return parts


def per_device(inputs, cotangent, right_factor, left_factor, norm_gain):
    core, yh, yl = lax.axis_index("c"), lax.axis_index("yh"), lax.axis_index("yl")
    place = jnp.stack([core, yh, lax.axis_index("x"), lax.axis_index("z"), 2 * yh + yl]).astype(jnp.int32)
    right = right_factor[0]
    left = left_factor[0]
    gain = norm_gain.reshape(2, 1, BS)

    keep, send = call(prep_kernel, place, (right, left, gain), (kept(2, BS, BS),) * 2)
    mine = jnp.stack([keep, swapped(send)])
    stage = kept(2, 4, BS, BS)
    part = kept(8, BS, BS)
    all_right, all_left = call(gather_y_kernel, place, gathered(mine, YS), (part, part))
    firsts = call(
        gather_pair_kernel, place, ring_gathered(all_right, "z") + ring_gathered(all_left, "x"), (kept(32, BS, BS),) * 2
    )
    rights, lefts = ring_gathered(firsts[0], "x"), ring_gathered(firsts[1], "z")

    x, grad, st = pl.pallas_call(
        tokens_kernel,
        out_shape=(ACT, ACT, STATS),
        grid_spec=pltpu.PrefetchScalarGridSpec(
            num_scalar_prefetch=1, grid=(GRID,), in_specs=[TOKENS_SPEC] * 2, out_specs=(WHOLE,) * 3
        ),
        compiler_params=pltpu.CompilerParams(vmem_limit_bytes=VMEM_LIMIT),
    )(place, inputs, cotangent)

    uo, us, st = call(start_kernel, place, (x, st, *rights), U_OUT, SCRATCH)
    xs, slopes, perms, rmss = [x], [], [], []
    for layer in range(3):
        xn, slope, perm, rms, uo, us, st = call(
            functools.partial(forward_kernel, layer), place,
            (uo, swapped(us), st, xs[-1], *lefts, *rights),
            (ACT, ACT, ACT, STATS) + U_OUT, SCRATCH,
        )
        xs.append(xn)
        slopes.append(slope)
        perms.append(perm)
        rmss.append(rms)
    rms, perm, pre, uo, us, st = call(
        functools.partial(turn_kernel, 3), place, (uo, swapped(us), st, grad, *lefts), (STATS, ACT, ACT) + U_OUT, SCRATCH
    )
    perms.append(perm)
    rmss.append(rms)
    slabs = {"right": (), "left": ()}

    def factors(right_layer, left_layer, ins):
        sides = [side for side, layer in (("right", right_layer), ("left", left_layer)) if layer is not None]
        old, aliases = [], {}
        for n, side in enumerate(sides):
            for k, slab in enumerate(slabs[side]):
                aliases[len(old)] = 4 * n + k
                old.append(slab)
        outs = call_into(
            functools.partial(factor_kernel, right_layer, left_layer, len(old)), place, ins, (SLAB,) * (4 * len(sides)), (), old,
            aliases,
        )
        for n, side in enumerate(sides):
            slabs[side] = outs[4 * n : 4 * n + 4]

    factors(None, 3, (perm, pre))
    for layer in (3, 2, 1):
        below = layer - 1
        go, gr = uo, swapped(us)
        pre, uo, us, st, *grad = call(
            functools.partial(backward_kernel, layer), place,
            (go, gr, st, rmss[layer], rmss[below], xs[layer], *([grad] if layer == 3 else grad), slopes[below], perms[below],
             *rights, *lefts),
            (ACT,) + U_OUT + (ACT,) * (layer > 1), SCRATCH,
        )
        factors(layer, below, (go, gr, xs[layer], perms[below], pre))
    factors(0, None, (uo, swapped(us), xs[0]))
    outs = call(sum_pair_kernel, place, ring_reduced(slabs["right"], slabs["left"], place), (stage,) * 8)
    parts = scattered(outs[:4], "z") + scattered(outs[4:], "x")
    outs = call(sum_ring_kernel, place, parts, (kept(2, 2, BS, BS),) * 4)
    sums = kept(2, BS, BS, dtype=F32)
    keep, send = call(sum_y_kernel, place, scattered(outs, YS), (sums, sums))
    whole = jax.ShapeDtypeStruct((2, BS, BS), F32)
    grad_right, grad_left, grad_gain = call(
        finish_kernel, place, (keep, swapped(send), right, gain), (whole, whole, jax.ShapeDtypeStruct((2, 1, BS), F32))
    )
    return grad_right[None], grad_left[None], grad_gain.reshape(1, 2 * BS)


def call_into(kernel, place, ins, outs, scratch, old, aliases):
    vmem = [pltpu.with_memory_space_constraint(a, pltpu.VMEM) for a in (*old, *ins)]
    operands = (*vmem[: len(old)], place, *vmem[len(old) :])
    return pl.pallas_call(
        kernel,
        out_shape=outs,
        in_specs=[WHOLE] * len(old) + [SCALARS] + [WHOLE] * len(ins),
        out_specs=(WHOLE,) * len(outs),
        scratch_shapes=scratch,
        input_output_aliases=aliases,
        compiler_params=pltpu.CompilerParams(vmem_limit_bytes=VMEM_LIMIT),
    )(*operands)


def solution(mesh):
    parts = Mesh(mesh.devices.reshape(2, 2, 4, 4, 2), ("yh", "c", "x", "z", "yl"))
    pipe, fsdp = ("yh", "c"), ("x", "z", "yl")
    return jax.shard_map(
        per_device,
        mesh=parts,
        in_specs=(P(None, fsdp, None), P(None, fsdp, None), P(pipe, fsdp, None, None), P(pipe, fsdp, None, None), P(pipe, fsdp)),
        out_specs=(P(pipe, fsdp, None, None), P(pipe, fsdp, None, None), P(pipe, fsdp)),
        check_vma=False,
    )
```

```python
import functools

import jax
import jax.numpy as jnp
from jax import lax
from jax.experimental import pallas as pl
from jax.experimental.pallas import tpu as pltpu
from jax.sharding import Mesh, PartitionSpec as P

EPSILON = 1e-05
TANH_SLOPE = 0.7978845608028654
CUBIC_TERM = 0.044715

BF = jnp.bfloat16
F32 = jnp.float32
HI = lax.Precision.HIGHEST
SWAP = ((0, 1), (1, 0))
YS = ("yh", "yl")
VMEM_LIMIT = 24 * 1024 * 1024

NB = 64
BS = 128
D = NB * BS
HB = NB // 2
ROWS = HB * BS
HALF = ROWS // 2
TOK = 128
STAT = 16
FORWARD = (65, 64)
BACKWARD = (33, 32)
GRID = 4
BPC = HB // GRID


def mm(a, b):
    return lax.dot_general(a, b, (((1,), (0,)), ((), ())), preferred_element_type=F32)


def mm_ta(a, b):
    return mm(a.T, b)


def mm_tb(a, b):
    return mm(a, b.T)


def mm_exact(a, b, dims=((1,), (0,))):
    return lax.dot_general(a, b, (dims, ((), ())), precision=HI, preferred_element_type=F32)


def iota2(dim):
    return lax.broadcasted_iota(jnp.int32, (BS, BS), dim)


def column_source(dp, q):
    rel = dp // 64
    return ((dp // 32) % 2) * 64 + 2 * (dp % 32) + (rel + q - 2 * rel * q)


def row_source(cp, q):
    rel = cp // 64
    return 4 * ((cp % 64) // 2) + 2 * (rel + q - 2 * rel * q) + cp % 2


def stat_rows(value):
    hi = value.astype(BF)
    rest = value - hi.astype(F32)
    mid = rest.astype(BF)
    lo = (rest - mid.astype(F32)).astype(BF)
    row = lax.broadcasted_iota(jnp.int32, (STAT, TOK), 0)
    out = jnp.where(row == 0, hi.astype(F32), jnp.where(row == 1, mid.astype(F32), lo.astype(F32)))
    return jnp.where(row < 3, out, 0.0).astype(BF)


def stat_total(own_ref, recv_ref):
    rows = recv_ref[pl.ds(HALF, STAT), :].astype(F32)
    return own_ref[0:1, :] + jnp.sum(rows, axis=0, keepdims=True)


def folded(value):
    return jnp.sum(value.reshape(BS // 8, 8, TOK), axis=0)


def back(index, steps):
    return (index + (4 - steps)) % 4


def blocks(place_ref):
    for sx in range(4):
        xm = back(place_ref[2], sx)
        for sz in range(4):
            zm = back(place_ref[3], sz)
            for ym in range(2):
                yield sx, sz, xm, zm, ym, xm * 8 + zm * 2 + ym


def slot(layer, at, yl):
    return layer * 8 + at * 2 + yl


def rows_of(m):
    return pl.ds(pl.multiple_of(m * BS, BS), BS)


def prep_kernel(place_ref, right_ref, left_ref, gain_ref, keep_ref, send_ref):
    core = place_ref[0]
    for dst, q in ((keep_ref, core), (send_ref, 1 - core)):
        gain_row = gain_ref[q].astype(F32)
        diag = jnp.where(iota2(0) == iota2(1), gain_row, 0.0).astype(BF)
        scaled = mm(diag, right_ref[q]).astype(BF)
        pick = (iota2(0) == column_source(iota2(1), q)).astype(F32).astype(BF)
        dst[0] = mm(scaled, pick).astype(BF)
        pick = (iota2(1) == row_source(iota2(0), q)).astype(F32).astype(BF)
        dst[1] = mm(pick, left_ref[q]).astype(BF)


def taken(pieces, s, k, size, at):
    if s == 2:
        return pieces[2 + k // 2][(k // 2) * (size // 8) + (k % 2) * size + at]
    return pieces[s + s // 3][k * size + at]


def gather_y_kernel(place_ref, p0, p1, p2, p3, right_ref, left_ref):
    core = place_ref[0]
    for s, piece in enumerate((p0, p1, p2, p3)):
        y = back(place_ref[4], s)
        for k in range(2):
            layer = (y // 2) * 2 + (core + k) % 2
            right_ref[layer * 2 + y % 2] = piece[k, 0]
            left_ref[layer * 2 + y % 2] = piece[k, 1]


def gather_pair_kernel(place_ref, *refs):
    for pieces, index, out in ((refs[:5], 3, refs[10]), (refs[5:10], 2, refs[11])):
        for s in range(4):
            at = back(place_ref[index], s)
            for k in range(4):
                for yl in range(2):
                    out[k * 8 + at * 2 + yl] = taken(pieces, s, k, 2, yl)


def tokens_kernel(place_ref, in_ref, cot_ref, x_ref, grad_ref, stat_ref):
    core = place_ref[0]
    base = pl.program_id(0) * BPC
    total = jnp.zeros((8, TOK), F32)
    for i in range(BPC):
        lanes = pl.ds(pl.multiple_of((2 * i + core) * BS, BS), BS)
        x = in_ref[:, :, lanes].reshape(TOK, BS).astype(F32).T
        x_ref[rows_of(base + i), :] = x.astype(BF)
        total = total + folded(x * x)
        grad_ref[rows_of(base + i), :] = cot_ref[:, :, lanes].reshape(TOK, BS).astype(F32).T.astype(BF)
    total = jnp.broadcast_to(jnp.sum(total, axis=0, keepdims=True), (8, TOK))

    @pl.when(pl.program_id(0) == 0)
    def _():
        stat_ref[...] = jnp.zeros_like(stat_ref)

    stat_ref[...] += total


def put_forward(scr, m, product):
    for part in range(2):
        for h in range(2):
            scr[part, pl.ds(m * 2 + h, 32, stride=FORWARD[0]), :] = product[part * 64 + h * 32 :][:32]


def put_backward(scr, m, product):
    for part in range(2):
        scr[part, pl.ds(m, 64, stride=BACKWARD[0]), :] = product[part * 64 :][:64]


def flush(runs, scr, total, own_ref, send_ref, stat_ref):
    pitch, used = runs
    for i in range(HALF // used):
        own_ref[pl.ds(i * used, used), :] = scr[0, pl.ds(i * pitch, used), :].astype(BF)
        send_ref[pl.ds(i * used, used), :] = scr[1, pl.ds(i * pitch, used), :].astype(BF)
    send_ref[pl.ds(HALF, STAT), :] = stat_rows(total)
    stat_ref[...] = jnp.broadcast_to(total, stat_ref.shape)


def gelu_parts(v):
    sq = v * v
    t = jnp.tanh(v * (TANH_SLOPE + (TANH_SLOPE * CUBIC_TERM) * sq))
    half = 0.5 * t + 0.5
    slope = half + (v * (1.0 - t * t)) * (0.5 * TANH_SLOPE + (1.5 * TANH_SLOPE * CUBIC_TERM) * sq)
    return v * half, slope


def rms_of(own_stat, recv_ref):
    return lax.rsqrt(stat_total(own_stat, recv_ref) * (1.0 / D) + EPSILON)


def permuted_block(own_ref, recv_ref, m, rms):
    rows = pl.ds(pl.multiple_of(m * 64, 64), 64)
    both = jnp.concatenate([own_ref[rows, :], recv_ref[rows, :]], axis=0)
    if rms is None:
        return both
    return (both.astype(F32) * rms).astype(BF)


def start_kernel(place_ref, x_ref, st_ref, w0, w1, w2, w3, w4, own_ref, send_ref, stat_ref, scr):
    rights = (w0, w1, w2, w3, w4)
    for sx, sz, xm, zm, ym, m in blocks(place_ref):
        put_forward(scr, m, mm_ta(taken(rights, sx, 0, 8, zm * 2 + ym), x_ref[rows_of(m), :]))
    flush(FORWARD, scr, st_ref[0:1, :], own_ref, send_ref, stat_ref)


def forward_kernel(
    layer, place_ref, uo_ref, ur_ref, us_ref, x_ref, l0, l1, l2, l3, l4, w0, w1, w2, w3, w4,
    xn_ref, slope_ref, perm_ref, rms_ref, own_ref, send_ref, stat_ref, scr,
):
    lefts, rights = (l0, l1, l2, l3, l4), (w0, w1, w2, w3, w4)
    rms = rms_of(us_ref, ur_ref)
    rms_ref[...] = jnp.broadcast_to(rms, rms_ref.shape)
    total = jnp.zeros((8, TOK), F32)
    for sx, sz, xm, zm, ym, m in blocks(place_ref):
        rows = rows_of(m)
        perm = permuted_block(uo_ref, ur_ref, m, rms)
        perm_ref[rows, :] = perm
        value, slope = gelu_parts(mm_ta(taken(lefts, sz, layer, 8, xm * 2 + ym), perm))
        slope_ref[rows, :] = slope.astype(BF)
        xb = (x_ref[rows, :].astype(F32) + value).astype(BF)
        xn_ref[rows, :] = xb
        x = xb.astype(F32)
        total = total + folded(x * x)
        put_forward(scr, m, mm_ta(taken(rights, sx, layer + 1, 8, zm * 2 + ym), xb))
    flush(FORWARD, scr, jnp.sum(total, axis=0, keepdims=True), own_ref, send_ref, stat_ref)


def left_chain(grad, slope, perm, left, rms, m, scr):
    grad_pre = (grad.astype(F32) * slope).astype(BF)
    grad_perm = mm(left, grad_pre)
    put_backward(scr, m, grad_perm * rms)
    return grad_pre, folded(grad_perm * perm.astype(F32))


def turn_kernel(
    layer, place_ref, uo_ref, ur_ref, us_ref, grad_ref, l0, l1, l2, l3, l4,
    rms_ref, perm_ref, pre_ref, own_ref, send_ref, stat_ref, scr,
):
    lefts = (l0, l1, l2, l3, l4)
    rms = rms_of(us_ref, ur_ref)
    rms_ref[...] = jnp.broadcast_to(rms, rms_ref.shape)
    total = jnp.zeros((8, TOK), F32)
    for sx, sz, xm, zm, ym, m in blocks(place_ref):
        rows = rows_of(m)
        perm = permuted_block(uo_ref, ur_ref, m, rms)
        perm_ref[rows, :] = perm
        left = taken(lefts, sz, layer, 8, xm * 2 + ym)
        slope = gelu_parts(mm_ta(left, perm))[1]
        pre_ref[rows, :], add = left_chain(grad_ref[rows, :], slope, perm, left, rms, m, scr)
        total = total + add
    flush(BACKWARD, scr, jnp.sum(total, axis=0, keepdims=True), own_ref, send_ref, stat_ref)


def backward_kernel(layer, *refs):
    place_ref, go_ref, gr_ref, gs_ref, rms_ref, rms_below_ref, x_ref, grad_ref, slope_ref, perm_ref = refs[:10]
    rights, lefts, refs = refs[10:15], refs[15:20], refs[20:]
    pre_ref, own_ref, send_ref, stat_ref = refs[:4]
    new_ref, scr = refs[4] if layer > 1 else None, refs[-1]
    below = layer - 1
    rms = rms_ref[0:1, :]
    rms_below = rms_below_ref[0:1, :]
    coef = stat_total(gs_ref, gr_ref) * (rms * rms * (1.0 / D))
    total = jnp.zeros((8, TOK), F32)
    for sx, sz, xm, zm, ym, m in blocks(place_ref):
        rows = rows_of(m)
        gf = permuted_block(go_ref, gr_ref, m, None)
        grad = grad_ref[rows, :].astype(F32) + mm(taken(rights, sx, layer, 8, zm * 2 + ym), gf)
        grad = (grad - x_ref[rows, :].astype(F32) * coef).astype(BF)
        if new_ref is not None:
            new_ref[rows, :] = grad
        left = taken(lefts, sz, below, 8, xm * 2 + ym)
        pre_ref[rows, :], add = left_chain(
            grad, slope_ref[rows, :].astype(F32), perm_ref[rows, :], left, rms_below, m, scr
        )
        total = total + add
    flush(BACKWARD, scr, jnp.sum(total, axis=0, keepdims=True), own_ref, send_ref, stat_ref)


def factor_kernel(right_layer, left_layer, n_old, *refs):
    refs = refs[n_old:]
    place_ref, refs = refs[0], refs[1:]
    if right_layer is not None:
        (go_ref, gr_ref, x_ref), refs = refs[:3], refs[3:]
    if left_layer is not None:
        (perm_ref, pre_ref), refs = refs[:2], refs[2:]
    for sx, sz, xm, zm, ym, m in blocks(place_ref):
        rows = rows_of(m)
        if right_layer is not None:
            gf = permuted_block(go_ref, gr_ref, m, None)
            refs[sx][slot(right_layer, zm, ym)] = mm_tb(x_ref[rows, :], gf).astype(BF)
        if left_layer is not None:
            refs[sz - 4][slot(left_layer, xm, ym)] = mm_tb(perm_ref[rows, :], pre_ref[rows, :]).astype(BF)


def added(parts):
    parts = [p.astype(F32) for p in parts]
    total = parts[0] + parts[1]
    return total + parts[2] if len(parts) == 3 else total + (parts[2] + parts[3]) if len(parts) == 4 else total


def pass_kernel(place_ref, down_ref, up_ref, lo_ref, hi_ref, down_out, up_out):
    del place_ref
    for i in range(16):
        down_out[i] = added((down_ref[i], lo_ref[i])).astype(BF)
        down_out[16 + i] = down_ref[16 + i]
        up_out[i] = up_ref[i]
        up_out[16 + i] = added((up_ref[16 + i], hi_ref[i])).astype(BF)


def sum_pair_kernel(place_ref, *refs):
    sources, outs = refs[:6], refs[6:]
    for side, index in ((0, 3), (1, 2)):
        slabs = sources[side * 3 :][:3]
        for s in range(4):
            at = back(place_ref[index], s)
            for yl in range(2):
                for layer in range(4):
                    outs[side * 4 + s][yl, layer] = added([t[slot(layer, at, yl)] for t in slabs]).astype(BF)


def sum_ring_kernel(place_ref, *refs):
    sources, outs = refs[:8], refs[8:]
    for side in range(2):
        slabs = sources[side * 4 :][:4]
        for s in range(4):
            y = back(place_ref[4], s)
            for k in range(2):
                outs[s][k, side] = added([t[y % 2, (y // 2) * 2 + k] for t in slabs]).astype(BF)


def sum_y_kernel(place_ref, p0, p1, p2, p3, keep_ref, send_ref):
    core = place_ref[0]
    for dst, k in ((keep_ref, core), (send_ref, 1 - core)):
        for side in range(2):
            dst[side] = added([t[k, side] for t in (p0, p1, p2, p3)])


def finish_kernel(place_ref, keep_ref, recv_ref, right_ref, gain_ref, gr_ref, gl_ref, gg_ref):
    core = place_ref[0]
    for src, q in ((keep_ref, core), (recv_ref, 1 - core)):
        pick = (iota2(1) == column_source(iota2(0), q)).astype(F32)
        raw = mm_exact(src[0], pick)
        diag = jnp.where(iota2(0) == iota2(1), gain_ref[q].astype(F32), 0.0)
        gr_ref[q] = mm_exact(diag, raw)
        gg_ref[q] = mm_exact(jnp.ones((8, BS), F32), raw * right_ref[q].astype(F32), ((1,), (1,)))[0:1]
        pick = (iota2(0) == row_source(iota2(1), q)).astype(F32)
        gl_ref[q] = mm_exact(pick, src[1])


WHOLE = pl.BlockSpec(memory_space=pltpu.VMEM)
SCALARS = pl.BlockSpec(memory_space=pltpu.SMEM)
ANY = pl.BlockSpec(memory_space=pl.ANY)
TOKENS_SPEC = pl.BlockSpec((2, 64, D // GRID), lambda g, place: (place[1], 0, g))


def kept(*shape, dtype=BF):
    return pltpu.VMEM(shape, dtype)


U_OUT = (kept(HALF, TOK), kept(HALF + STAT, TOK), kept(8, TOK, dtype=F32))
ACT = kept(ROWS, TOK)
STATS = kept(8, TOK, dtype=F32)
SLAB = kept(32, BS, BS)
SCRATCH = (pltpu.VMEM((2, HALF + 64, TOK), F32),)


def call(kernel, place, ins, outs, scratch=(), old=()):
    vmem = [pltpu.with_memory_space_constraint(a, pltpu.VMEM) for a in (*old, *ins)]
    ins = (*vmem[: len(old)], place, *vmem[len(old) :])
    return pl.pallas_call(
        kernel,
        out_shape=outs,
        in_specs=[WHOLE] * len(old) + [SCALARS] + [WHOLE] * (len(ins) - len(old) - 1),
        out_specs=(WHOLE,) * len(outs),
        scratch_shapes=scratch,
        compiler_params=pltpu.CompilerParams(vmem_limit_bytes=VMEM_LIMIT),
    )(*ins)


def swapped(value):
    return lax.ppermute(value, "c", SWAP)


def ring(value, axes, steps):
    return lax.ppermute(value, axes, [(i, (i + steps) % 4) for i in range(4)])


def gathered(value, axes):
    return [value] + [ring(value, axes, s) for s in (1, 2, 3)]


def ring_gathered(value, axes):
    half = value.shape[0] // 2
    up, down = ring(value, axes, 1), ring(value, axes, -1)
    spare = half // 16
    return [value, up, ring(up[: half + spare], axes, 1), ring(down[half - spare :], axes, -1), down]


def scattered(slabs, axes):
    return [slabs[0]] + [ring(slabs[s], axes, -s) for s in (1, 2, 3)]


def ring_reduced(right_slabs, left_slabs, place):
    sides = ((right_slabs, "x"), (left_slabs, "z"))
    far = [(ring(slabs[2][:16], axes, -1), ring(slabs[2][16:], axes, 1)) for slabs, axes in sides]
    parts = []
    for (slabs, axes), got in zip(sides, far):
        down, up = call(pass_kernel, place, (slabs[1], slabs[3], *got), (SLAB, SLAB))
        parts += [slabs[0], ring(down, axes, -1), ring(up, axes, 1)]
    return parts


def per_device(inputs, cotangent, right_factor, left_factor, norm_gain):
    core, yh, yl = lax.axis_index("c"), lax.axis_index("yh"), lax.axis_index("yl")
    place = jnp.stack([core, yh, lax.axis_index("x"), lax.axis_index("z"), 2 * yh + yl]).astype(jnp.int32)
    right = right_factor[0]
    left = left_factor[0]
    gain = norm_gain.reshape(2, 1, BS)

    keep, send = pl.pallas_call(
        prep_kernel,
        out_shape=(kept(2, BS, BS),) * 2,
        in_specs=[SCALARS] + [WHOLE] * 3,
        out_specs=(WHOLE,) * 2,
        compiler_params=pltpu.CompilerParams(vmem_limit_bytes=VMEM_LIMIT),
    )(place, right, left, gain)
    mine = jnp.stack([keep, swapped(send)])
    stage = kept(2, 4, BS, BS)
    part = kept(8, BS, BS)
    all_right, all_left = call(gather_y_kernel, place, gathered(mine, YS), (part, part))
    firsts = call(
        gather_pair_kernel, place, ring_gathered(all_right, "z") + ring_gathered(all_left, "x"), (kept(32, BS, BS),) * 2
    )
    rights, lefts = ring_gathered(firsts[0], "x"), ring_gathered(firsts[1], "z")

    x, grad, st = pl.pallas_call(
        tokens_kernel,
        out_shape=(ACT, ACT, STATS),
        grid_spec=pltpu.PrefetchScalarGridSpec(
            num_scalar_prefetch=1, grid=(GRID,), in_specs=[TOKENS_SPEC] * 2, out_specs=(WHOLE,) * 3
        ),
        compiler_params=pltpu.CompilerParams(vmem_limit_bytes=VMEM_LIMIT),
    )(place, inputs, cotangent)

    uo, us, st = call(start_kernel, place, (x, st, *rights), U_OUT, SCRATCH)
    xs, slopes, perms, rmss = [x], [], [], []
    for layer in range(3):
        xn, slope, perm, rms, uo, us, st = call(
            functools.partial(forward_kernel, layer), place,
            (uo, swapped(us), st, xs[-1], *lefts, *rights),
            (ACT, ACT, ACT, STATS) + U_OUT, SCRATCH,
        )
        xs.append(xn)
        slopes.append(slope)
        perms.append(perm)
        rmss.append(rms)
    rms, perm, pre, uo, us, st = call(
        functools.partial(turn_kernel, 3), place, (uo, swapped(us), st, grad, *lefts), (STATS, ACT, ACT) + U_OUT, SCRATCH
    )
    perms.append(perm)
    rmss.append(rms)
    slabs = {"right": (), "left": ()}

    def factors(right_layer, left_layer, ins):
        sides = [side for side, layer in (("right", right_layer), ("left", left_layer)) if layer is not None]
        old, aliases = [], {}
        for n, side in enumerate(sides):
            for k, slab in enumerate(slabs[side]):
                aliases[len(old)] = 4 * n + k
                old.append(slab)
        outs = call_into(
            functools.partial(factor_kernel, right_layer, left_layer, len(old)), place, ins, (SLAB,) * (4 * len(sides)), (), old,
            aliases,
        )
        for n, side in enumerate(sides):
            slabs[side] = outs[4 * n : 4 * n + 4]

    factors(None, 3, (perm, pre))
    for layer in (3, 2, 1):
        below = layer - 1
        go, gr = uo, swapped(us)
        go, slabs["left"] = lax.optimization_barrier((go, slabs["left"]))
        pre, uo, us, st, *grad = call(
            functools.partial(backward_kernel, layer), place,
            (go, gr, st, rmss[layer], rmss[below], xs[layer], *([grad] if layer == 3 else grad), slopes[below], perms[below],
             *rights, *lefts),
            (ACT,) + U_OUT + (ACT,) * (layer > 1), SCRATCH,
        )
        factors(layer, below, (go, gr, xs[layer], perms[below], pre))
    factors(0, None, (uo, swapped(us), xs[0]))
    outs = call(sum_pair_kernel, place, ring_reduced(slabs["right"], slabs["left"], place), (stage,) * 8)
    parts = scattered(outs[:4], "z") + scattered(outs[4:], "x")
    outs = call(sum_ring_kernel, place, parts, (kept(2, 2, BS, BS),) * 4)
    sums = kept(2, BS, BS, dtype=F32)
    keep, send = call(sum_y_kernel, place, scattered(outs, YS), (sums, sums))
    whole = jax.ShapeDtypeStruct((2, BS, BS), F32)
    grad_right, grad_left, grad_gain = call(
        finish_kernel, place, (keep, swapped(send), right, gain), (whole, whole, jax.ShapeDtypeStruct((2, 1, BS), F32))
    )
    return grad_right[None], grad_left[None], grad_gain.reshape(1, 2 * BS)


def call_into(kernel, place, ins, outs, scratch, old, aliases):
    vmem = [pltpu.with_memory_space_constraint(a, pltpu.VMEM) for a in (*old, *ins)]
    operands = (*vmem[: len(old)], place, *vmem[len(old) :])
    return pl.pallas_call(
        kernel,
        out_shape=outs,
        in_specs=[WHOLE] * len(old) + [SCALARS] + [WHOLE] * len(ins),
        out_specs=(WHOLE,) * len(outs),
        scratch_shapes=scratch,
        input_output_aliases=aliases,
        compiler_params=pltpu.CompilerParams(vmem_limit_bytes=VMEM_LIMIT),
    )(*operands)


def solution(mesh):
    parts = Mesh(mesh.devices.reshape(2, 2, 4, 4, 2), ("yh", "c", "x", "z", "yl"))
    pipe, fsdp = ("yh", "c"), ("x", "z", "yl")
    return jax.shard_map(
        per_device,
        mesh=parts,
        in_specs=(P(None, fsdp, None), P(None, fsdp, None), P(pipe, fsdp, None, None), P(pipe, fsdp, None, None), P(pipe, fsdp)),
        out_specs=(P(pipe, fsdp, None, None), P(pipe, fsdp, None, None), P(pipe, fsdp)),
        check_vma=False,
    )
```

```python
import functools

import jax
import jax.numpy as jnp
from jax import lax
from jax.experimental import pallas as pl
from jax.experimental.pallas import tpu as pltpu
from jax.sharding import Mesh, PartitionSpec as P

EPSILON = 1e-05
TANH_SLOPE = 0.7978845608028654
CUBIC_TERM = 0.044715

BF = jnp.bfloat16
F32 = jnp.float32
HI = lax.Precision.HIGHEST
SWAP = ((0, 1), (1, 0))
YS = ("yh", "yl")
VMEM_LIMIT = 24 * 1024 * 1024

NB = 64
BS = 128
D = NB * BS
HB = NB // 2
ROWS = HB * BS
HALF = ROWS // 2
TOK = 128
STAT = 16
FORWARD = (65, 64)
BACKWARD = (33, 32)
GRID = 4
BPC = HB // GRID


def mm(a, b):
    return lax.dot_general(a, b, (((1,), (0,)), ((), ())), preferred_element_type=F32)


def mm_ta(a, b):
    return mm(a.T, b)


def mm_tb(a, b):
    return mm(a, b.T)


def mm_exact(a, b, dims=((1,), (0,))):
    return lax.dot_general(a, b, (dims, ((), ())), precision=HI, preferred_element_type=F32)


def iota2(dim):
    return lax.broadcasted_iota(jnp.int32, (BS, BS), dim)


def column_source(dp, q):
    rel = dp // 64
    return ((dp // 32) % 2) * 64 + 2 * (dp % 32) + (rel + q - 2 * rel * q)


def row_source(cp, q):
    rel = cp // 64
    return 4 * ((cp % 64) // 2) + 2 * (rel + q - 2 * rel * q) + cp % 2


def stat_rows(value):
    hi = value.astype(BF)
    rest = value - hi.astype(F32)
    mid = rest.astype(BF)
    lo = (rest - mid.astype(F32)).astype(BF)
    row = lax.broadcasted_iota(jnp.int32, (STAT, TOK), 0)
    out = jnp.where(row == 0, hi.astype(F32), jnp.where(row == 1, mid.astype(F32), lo.astype(F32)))
    return jnp.where(row < 3, out, 0.0).astype(BF)


def stat_total(own_ref, recv_ref):
    rows = recv_ref[pl.ds(HALF, STAT), :].astype(F32)
    return own_ref[0:1, :] + jnp.sum(rows, axis=0, keepdims=True)


def folded(value):
    return jnp.sum(value.reshape(BS // 8, 8, TOK), axis=0)


def back(index, steps):
    return (index + (4 - steps)) % 4


def blocks(place_ref):
    for sx in range(4):
        xm = back(place_ref[2], sx)
        for sz in range(4):
            zm = back(place_ref[3], sz)
            for ym in range(2):
                yield sx, sz, xm, zm, ym, xm * 8 + zm * 2 + ym


def slot(layer, at, yl):
    return layer * 8 + at * 2 + yl


def rows_of(m):
    return pl.ds(pl.multiple_of(m * BS, BS), BS)


def prep_kernel(place_ref, right_ref, left_ref, gain_ref, keep_ref, send_ref):
    core = place_ref[0]
    for dst, q in ((keep_ref, core), (send_ref, 1 - core)):
        gain_row = gain_ref[q].astype(F32)
        diag = jnp.where(iota2(0) == iota2(1), gain_row, 0.0).astype(BF)
        scaled = mm(diag, right_ref[q]).astype(BF)
        pick = (iota2(0) == column_source(iota2(1), q)).astype(F32).astype(BF)
        dst[0] = mm(scaled, pick).astype(BF)
        pick = (iota2(1) == row_source(iota2(0), q)).astype(F32).astype(BF)
        dst[1] = mm(pick, left_ref[q]).astype(BF)


def taken(pieces, s, k, size, at):
    if s == 2:
        return pieces[2 + k // 2][(k // 2) * (size // 8) + (k % 2) * size + at]
    return pieces[s + s // 3][k * size + at]


def gather_y_kernel(place_ref, p0, p1, p2, p3, right_ref, left_ref):
    core = place_ref[0]
    for s, piece in enumerate((p0, p1, p2, p3)):
        y = back(place_ref[4], s)
        for k in range(2):
            layer = (y // 2) * 2 + (core + k) % 2
            right_ref[layer * 2 + y % 2] = piece[k, 0]
            left_ref[layer * 2 + y % 2] = piece[k, 1]


def gather_pair_kernel(place_ref, *refs):
    for pieces, index, out in ((refs[:5], 3, refs[10]), (refs[5:10], 2, refs[11])):
        for s in range(4):
            at = back(place_ref[index], s)
            for k in range(4):
                for yl in range(2):
                    out[k * 8 + at * 2 + yl] = taken(pieces, s, k, 2, yl)


def tokens_kernel(place_ref, in_ref, cot_ref, x_ref, grad_ref, stat_ref):
    core = place_ref[0]
    base = pl.program_id(0) * BPC
    total = jnp.zeros((8, TOK), F32)
    for i in range(BPC):
        lanes = pl.ds(pl.multiple_of((2 * i + core) * BS, BS), BS)
        x = in_ref[:, :, lanes].reshape(TOK, BS).astype(F32).T
        x_ref[rows_of(base + i), :] = x.astype(BF)
        total = total + folded(x * x)
        grad_ref[rows_of(base + i), :] = cot_ref[:, :, lanes].reshape(TOK, BS).astype(F32).T.astype(BF)
    total = jnp.broadcast_to(jnp.sum(total, axis=0, keepdims=True), (8, TOK))

    @pl.when(pl.program_id(0) == 0)
    def _():
        stat_ref[...] = jnp.zeros_like(stat_ref)

    stat_ref[...] += total


def put_forward(scr, m, product):
    for part in range(2):
        for h in range(2):
            scr[part, pl.ds(m * 2 + h, 32, stride=FORWARD[0]), :] = product[part * 64 + h * 32 :][:32]


def put_backward(scr, m, product):
    for part in range(2):
        scr[part, pl.ds(m, 64, stride=BACKWARD[0]), :] = product[part * 64 :][:64]


def flush(runs, scr, total, own_ref, send_ref, stat_ref):
    pitch, used = runs
    for i in range(HALF // used):
        own_ref[pl.ds(i * used, used), :] = scr[0, pl.ds(i * pitch, used), :].astype(BF)
        send_ref[pl.ds(i * used, used), :] = scr[1, pl.ds(i * pitch, used), :].astype(BF)
    send_ref[pl.ds(HALF, STAT), :] = stat_rows(total)
    stat_ref[...] = jnp.broadcast_to(total, stat_ref.shape)


def gelu_parts(v):
    sq = v * v
    t = jnp.tanh(v * (TANH_SLOPE + (TANH_SLOPE * CUBIC_TERM) * sq))
    half = 0.5 * t + 0.5
    slope = half + (v * (1.0 - t * t)) * (0.5 * TANH_SLOPE + (1.5 * TANH_SLOPE * CUBIC_TERM) * sq)
    return v * half, slope


def rms_of(own_stat, recv_ref):
    return lax.rsqrt(stat_total(own_stat, recv_ref) * (1.0 / D) + EPSILON)


def permuted_block(own_ref, recv_ref, m, rms):
    rows = pl.ds(pl.multiple_of(m * 64, 64), 64)
    both = jnp.concatenate([own_ref[rows, :], recv_ref[rows, :]], axis=0)
    if rms is None:
        return both
    return (both.astype(F32) * rms).astype(BF)


def start_kernel(place_ref, x_ref, st_ref, w0, w1, w2, w3, w4, own_ref, send_ref, stat_ref, scr):
    rights = (w0, w1, w2, w3, w4)
    for sx, sz, xm, zm, ym, m in blocks(place_ref):
        put_forward(scr, m, mm_ta(taken(rights, sx, 0, 8, zm * 2 + ym), x_ref[rows_of(m), :]))
    flush(FORWARD, scr, st_ref[0:1, :], own_ref, send_ref, stat_ref)


def forward_kernel(
    layer, place_ref, uo_ref, ur_ref, us_ref, x_ref, l0, l1, l2, l3, l4, w0, w1, w2, w3, w4,
    xn_ref, slope_ref, perm_ref, rms_ref, own_ref, send_ref, stat_ref, scr,
):
    lefts, rights = (l0, l1, l2, l3, l4), (w0, w1, w2, w3, w4)
    rms = rms_of(us_ref, ur_ref)
    rms_ref[...] = jnp.broadcast_to(rms, rms_ref.shape)
    total = jnp.zeros((8, TOK), F32)
    for sx, sz, xm, zm, ym, m in blocks(place_ref):
        rows = rows_of(m)
        perm = permuted_block(uo_ref, ur_ref, m, rms)
        perm_ref[rows, :] = perm
        value, slope = gelu_parts(mm_ta(taken(lefts, sz, layer, 8, xm * 2 + ym), perm))
        slope_ref[rows, :] = slope.astype(BF)
        xb = (x_ref[rows, :].astype(F32) + value).astype(BF)
        xn_ref[rows, :] = xb
        x = xb.astype(F32)
        total = total + folded(x * x)
        put_forward(scr, m, mm_ta(taken(rights, sx, layer + 1, 8, zm * 2 + ym), xb))
    flush(FORWARD, scr, jnp.sum(total, axis=0, keepdims=True), own_ref, send_ref, stat_ref)


def left_chain(grad, slope, perm, left, rms, m, scr):
    grad_pre = (grad.astype(F32) * slope).astype(BF)
    grad_perm = mm(left, grad_pre)
    put_backward(scr, m, grad_perm * rms)
    return grad_pre, folded(grad_perm * perm.astype(F32))


def turn_kernel(
    layer, place_ref, uo_ref, ur_ref, us_ref, grad_ref, l0, l1, l2, l3, l4,
    rms_ref, perm_ref, pre_ref, own_ref, send_ref, stat_ref, scr,
):
    lefts = (l0, l1, l2, l3, l4)
    rms = rms_of(us_ref, ur_ref)
    rms_ref[...] = jnp.broadcast_to(rms, rms_ref.shape)
    total = jnp.zeros((8, TOK), F32)
    for sx, sz, xm, zm, ym, m in blocks(place_ref):
        rows = rows_of(m)
        perm = permuted_block(uo_ref, ur_ref, m, rms)
        perm_ref[rows, :] = perm
        left = taken(lefts, sz, layer, 8, xm * 2 + ym)
        slope = gelu_parts(mm_ta(left, perm))[1]
        pre_ref[rows, :], add = left_chain(grad_ref[rows, :], slope, perm, left, rms, m, scr)
        total = total + add
    flush(BACKWARD, scr, jnp.sum(total, axis=0, keepdims=True), own_ref, send_ref, stat_ref)


def backward_kernel(layer, *refs):
    place_ref, go_ref, gr_ref, gs_ref, rms_ref, rms_below_ref, x_ref, grad_ref, slope_ref, perm_ref = refs[:10]
    rights, lefts, refs = refs[10:15], refs[15:20], refs[20:]
    pre_ref, own_ref, send_ref, stat_ref = refs[:4]
    new_ref, scr = refs[4] if layer > 1 else None, refs[-1]
    below = layer - 1
    rms = rms_ref[0:1, :]
    rms_below = rms_below_ref[0:1, :]
    coef = stat_total(gs_ref, gr_ref) * (rms * rms * (1.0 / D))
    total = jnp.zeros((8, TOK), F32)
    for sx, sz, xm, zm, ym, m in blocks(place_ref):
        rows = rows_of(m)
        gf = permuted_block(go_ref, gr_ref, m, None)
        grad = grad_ref[rows, :].astype(F32) + mm(taken(rights, sx, layer, 8, zm * 2 + ym), gf)
        grad = (grad - x_ref[rows, :].astype(F32) * coef).astype(BF)
        if new_ref is not None:
            new_ref[rows, :] = grad
        left = taken(lefts, sz, below, 8, xm * 2 + ym)
        pre_ref[rows, :], add = left_chain(
            grad, slope_ref[rows, :].astype(F32), perm_ref[rows, :], left, rms_below, m, scr
        )
        total = total + add
    flush(BACKWARD, scr, jnp.sum(total, axis=0, keepdims=True), own_ref, send_ref, stat_ref)


def factor_kernel(right_layer, left_layer, n_old, *refs):
    refs = refs[n_old:]
    place_ref, refs = refs[0], refs[1:]
    if right_layer is not None:
        (go_ref, gr_ref, x_ref), refs = refs[:3], refs[3:]
    if left_layer is not None:
        (perm_ref, pre_ref), refs = refs[:2], refs[2:]
    for sx, sz, xm, zm, ym, m in blocks(place_ref):
        rows = rows_of(m)
        if right_layer is not None:
            gf = permuted_block(go_ref, gr_ref, m, None)
            refs[sx][slot(right_layer, zm, ym)] = mm_tb(x_ref[rows, :], gf).astype(BF)
        if left_layer is not None:
            refs[sz - 4][slot(left_layer, xm, ym)] = mm_tb(perm_ref[rows, :], pre_ref[rows, :]).astype(BF)


def added(parts):
    parts = [p.astype(F32) for p in parts]
    total = parts[0] + parts[1]
    return total + parts[2] if len(parts) == 3 else total + (parts[2] + parts[3]) if len(parts) == 4 else total


def pass_kernel(place_ref, down_ref, up_ref, lo_ref, hi_ref, down_out, up_out):
    del place_ref
    for i in range(16):
        down_out[i] = added((down_ref[i], lo_ref[i])).astype(BF)
        down_out[16 + i] = down_ref[16 + i]
        up_out[i] = up_ref[i]
        up_out[16 + i] = added((up_ref[16 + i], hi_ref[i])).astype(BF)


def sum_pair_kernel(place_ref, *refs):
    sources, outs = refs[:6], refs[6:]
    for side, index in ((0, 3), (1, 2)):
        slabs = sources[side * 3 :][:3]
        for s in range(4):
            at = back(place_ref[index], s)
            for yl in range(2):
                for layer in range(4):
                    outs[side * 4 + s][yl, layer] = added([t[slot(layer, at, yl)] for t in slabs]).astype(BF)


def sum_ring_kernel(place_ref, *refs):
    sources, outs = refs[:8], refs[8:]
    for side in range(2):
        slabs = sources[side * 4 :][:4]
        for s in range(4):
            y = back(place_ref[4], s)
            for k in range(2):
                outs[s][k, side] = added([t[y % 2, (y // 2) * 2 + k] for t in slabs]).astype(BF)


def sum_y_kernel(place_ref, p0, p1, p2, p3, keep_ref, send_ref):
    core = place_ref[0]
    for dst, k in ((keep_ref, core), (send_ref, 1 - core)):
        for side in range(2):
            dst[side] = added([t[k, side] for t in (p0, p1, p2, p3)])


def finish_kernel(place_ref, keep_ref, recv_ref, right_ref, gain_ref, gr_ref, gl_ref, gg_ref):
    core = place_ref[0]
    for src, q in ((keep_ref, core), (recv_ref, 1 - core)):
        pick = (iota2(1) == column_source(iota2(0), q)).astype(F32)
        raw = mm_exact(src[0], pick)
        diag = jnp.where(iota2(0) == iota2(1), gain_ref[q].astype(F32), 0.0)
        gr_ref[q] = mm_exact(diag, raw)
        gg_ref[q] = mm_exact(jnp.ones((8, BS), F32), raw * right_ref[q].astype(F32), ((1,), (1,)))[0:1]
        pick = (iota2(0) == row_source(iota2(1), q)).astype(F32)
        gl_ref[q] = mm_exact(pick, src[1])


WHOLE = pl.BlockSpec(memory_space=pltpu.VMEM)
SCALARS = pl.BlockSpec(memory_space=pltpu.SMEM)
ANY = pl.BlockSpec(memory_space=pl.ANY)
TOKENS_SPEC = pl.BlockSpec((2, 64, D // GRID), lambda g, place: (place[1], 0, g))


def kept(*shape, dtype=BF):
    return pltpu.VMEM(shape, dtype)


U_OUT = (kept(HALF, TOK), kept(HALF + STAT, TOK), kept(8, TOK, dtype=F32))
ACT = kept(ROWS, TOK)
STATS = kept(8, TOK, dtype=F32)
SLAB = kept(32, BS, BS)
SCRATCH = (pltpu.VMEM((2, HALF + 128, TOK), F32),)


def call(kernel, place, ins, outs, scratch=(), old=()):
    vmem = [pltpu.with_memory_space_constraint(a, pltpu.VMEM) for a in (*old, *ins)]
    ins = (*vmem[: len(old)], place, *vmem[len(old) :])
    return pl.pallas_call(
        kernel,
        out_shape=outs,
        in_specs=[WHOLE] * len(old) + [SCALARS] + [WHOLE] * (len(ins) - len(old) - 1),
        out_specs=(WHOLE,) * len(outs),
        scratch_shapes=scratch,
        compiler_params=pltpu.CompilerParams(vmem_limit_bytes=VMEM_LIMIT),
    )(*ins)


def swapped(value):
    return lax.ppermute(value, "c", SWAP)


def ring(value, axes, steps):
    return lax.ppermute(value, axes, [(i, (i + steps) % 4) for i in range(4)])


def gathered(value, axes):
    return [value] + [ring(value, axes, s) for s in (1, 2, 3)]


def ring_gathered(value, axes):
    half = value.shape[0] // 2
    up, down = ring(value, axes, 1), ring(value, axes, -1)
    spare = half // 16
    return [value, up, ring(up[: half + spare], axes, 1), ring(down[half - spare :], axes, -1), down]


def scattered(slabs, axes):
    return [slabs[0]] + [ring(slabs[s], axes, -s) for s in (1, 2, 3)]


def ring_reduced(right_slabs, left_slabs, place):
    sides = ((right_slabs, "x"), (left_slabs, "z"))
    far = [(ring(slabs[2][:16], axes, -1), ring(slabs[2][16:], axes, 1)) for slabs, axes in sides]
    parts = []
    for (slabs, axes), got in zip(sides, far):
        down, up = call(pass_kernel, place, (slabs[1], slabs[3], *got), (SLAB, SLAB))
        parts += [slabs[0], ring(down, axes, -1), ring(up, axes, 1)]
    return parts


def per_device(inputs, cotangent, right_factor, left_factor, norm_gain):
    core, yh, yl = lax.axis_index("c"), lax.axis_index("yh"), lax.axis_index("yl")
    place = jnp.stack([core, yh, lax.axis_index("x"), lax.axis_index("z"), 2 * yh + yl]).astype(jnp.int32)
    right = right_factor[0]
    left = left_factor[0]
    gain = norm_gain.reshape(2, 1, BS)

    keep, send = pl.pallas_call(
        prep_kernel,
        out_shape=(kept(2, BS, BS),) * 2,
        in_specs=[SCALARS] + [WHOLE] * 3,
        out_specs=(WHOLE,) * 2,
        compiler_params=pltpu.CompilerParams(vmem_limit_bytes=VMEM_LIMIT),
    )(place, right, left, gain)
    mine = jnp.stack([keep, swapped(send)])
    stage = kept(2, 4, BS, BS)
    part = kept(8, BS, BS)
    all_right, all_left = call(gather_y_kernel, place, gathered(mine, YS), (part, part))
    firsts = call(
        gather_pair_kernel, place, ring_gathered(all_right, "z") + ring_gathered(all_left, "x"), (kept(32, BS, BS),) * 2
    )
    rights, lefts = ring_gathered(firsts[0], "x"), ring_gathered(firsts[1], "z")

    x, grad, st = pl.pallas_call(
        tokens_kernel,
        out_shape=(ACT, ACT, STATS),
        grid_spec=pltpu.PrefetchScalarGridSpec(
            num_scalar_prefetch=1, grid=(GRID,), in_specs=[TOKENS_SPEC] * 2, out_specs=(WHOLE,) * 3
        ),
        compiler_params=pltpu.CompilerParams(vmem_limit_bytes=VMEM_LIMIT),
    )(place, inputs, cotangent)

    uo, us, st = call(start_kernel, place, (x, st, *rights), U_OUT, SCRATCH)
    xs, slopes, perms, rmss = [x], [], [], []
    for layer in range(3):
        xn, slope, perm, rms, uo, us, st = call(
            functools.partial(forward_kernel, layer), place,
            (uo, swapped(us), st, xs[-1], *lefts, *rights),
            (ACT, ACT, ACT, STATS) + U_OUT, SCRATCH,
        )
        xs.append(xn)
        slopes.append(slope)
        perms.append(perm)
        rmss.append(rms)
    rms, perm, pre, uo, us, st = call(
        functools.partial(turn_kernel, 3), place, (uo, swapped(us), st, grad, *lefts), (STATS, ACT, ACT) + U_OUT, SCRATCH
    )
    perms.append(perm)
    rmss.append(rms)
    slabs = {"right": (), "left": ()}

    def factors(right_layer, left_layer, ins):
        sides = [side for side, layer in (("right", right_layer), ("left", left_layer)) if layer is not None]
        old, aliases = [], {}
        for n, side in enumerate(sides):
            for k, slab in enumerate(slabs[side]):
                aliases[len(old)] = 4 * n + k
                old.append(slab)
        outs = call_into(
            functools.partial(factor_kernel, right_layer, left_layer, len(old)), place, ins, (SLAB,) * (4 * len(sides)), (), old,
            aliases,
        )
        for n, side in enumerate(sides):
            slabs[side] = outs[4 * n : 4 * n + 4]

    factors(None, 3, (perm, pre))
    for layer in (3, 2, 1):
        below = layer - 1
        go, gr = uo, swapped(us)
        go, slabs["left"] = lax.optimization_barrier((go, slabs["left"]))
        pre, uo, us, st, *grad = call(
            functools.partial(backward_kernel, layer), place,
            (go, gr, st, rmss[layer], rmss[below], xs[layer], *([grad] if layer == 3 else grad), slopes[below], perms[below],
             *rights, *lefts),
            (ACT,) + U_OUT + (ACT,) * (layer > 1), SCRATCH,
        )
        factors(layer, below, (go, gr, xs[layer], perms[below], pre))
    factors(0, None, (uo, swapped(us), xs[0]))
    outs = call(sum_pair_kernel, place, ring_reduced(slabs["right"], slabs["left"], place), (stage,) * 8)
    parts = scattered(outs[:4], "z") + scattered(outs[4:], "x")
    outs = call(sum_ring_kernel, place, parts, (kept(2, 2, BS, BS),) * 4)
    sums = kept(2, BS, BS, dtype=F32)
    keep, send = call(sum_y_kernel, place, scattered(outs, YS), (sums, sums))
    whole = jax.ShapeDtypeStruct((2, BS, BS), F32)
    grad_right, grad_left, grad_gain = call(
        finish_kernel, place, (keep, swapped(send), right, gain), (whole, whole, jax.ShapeDtypeStruct((2, 1, BS), F32))
    )
    return grad_right[None], grad_left[None], grad_gain.reshape(1, 2 * BS)


def call_into(kernel, place, ins, outs, scratch, old, aliases):
    vmem = [pltpu.with_memory_space_constraint(a, pltpu.VMEM) for a in (*old, *ins)]
    operands = (*vmem[: len(old)], place, *vmem[len(old) :])
    return pl.pallas_call(
        kernel,
        out_shape=outs,
        in_specs=[WHOLE] * len(old) + [SCALARS] + [WHOLE] * len(ins),
        out_specs=(WHOLE,) * len(outs),
        scratch_shapes=scratch,
        input_output_aliases=aliases,
        compiler_params=pltpu.CompilerParams(vmem_limit_bytes=VMEM_LIMIT),
    )(*operands)


def solution(mesh):
    parts = Mesh(mesh.devices.reshape(2, 2, 4, 4, 2), ("yh", "c", "x", "z", "yl"))
    pipe, fsdp = ("yh", "c"), ("x", "z", "yl")
    return jax.shard_map(
        per_device,
        mesh=parts,
        in_specs=(P(None, fsdp, None), P(None, fsdp, None), P(pipe, fsdp, None, None), P(pipe, fsdp, None, None), P(pipe, fsdp)),
        out_specs=(P(pipe, fsdp, None, None), P(pipe, fsdp, None, None), P(pipe, fsdp)),
        check_vma=False,
    )
```

```python
import functools

import jax
import jax.numpy as jnp
from jax import lax
from jax.experimental import pallas as pl
from jax.experimental.pallas import tpu as pltpu
from jax.sharding import Mesh, PartitionSpec as P

EPSILON = 1e-05
TANH_SLOPE = 0.7978845608028654
CUBIC_TERM = 0.044715

BF = jnp.bfloat16
F32 = jnp.float32
HI = lax.Precision.HIGHEST
SWAP = ((0, 1), (1, 0))
YS = ("yh", "yl")
VMEM_LIMIT = 24 * 1024 * 1024

NB = 64
BS = 128
D = NB * BS
HB = NB // 2
ROWS = HB * BS
HALF = ROWS // 2
TOK = 128
STAT = 16
FORWARD = (65, 64)
BACKWARD = (33, 32)
GRID = 4
BPC = HB // GRID


def mm(a, b):
    return lax.dot_general(a, b, (((1,), (0,)), ((), ())), preferred_element_type=F32)


def mm_ta(a, b):
    return mm(a.T, b)


def mm_tb(a, b):
    return mm(a, b.T)


def mm_exact(a, b, dims=((1,), (0,))):
    return lax.dot_general(a, b, (dims, ((), ())), precision=HI, preferred_element_type=F32)


def iota2(dim):
    return lax.broadcasted_iota(jnp.int32, (BS, BS), dim)


def column_source(dp, q):
    rel = dp // 64
    return ((dp // 32) % 2) * 64 + 2 * (dp % 32) + (rel + q - 2 * rel * q)


def row_source(cp, q):
    rel = cp // 64
    return 4 * ((cp % 64) // 2) + 2 * (rel + q - 2 * rel * q) + cp % 2


def stat_rows(value):
    hi = value.astype(BF)
    rest = value - hi.astype(F32)
    mid = rest.astype(BF)
    lo = (rest - mid.astype(F32)).astype(BF)
    row = lax.broadcasted_iota(jnp.int32, (STAT, TOK), 0)
    out = jnp.where(row == 0, hi.astype(F32), jnp.where(row == 1, mid.astype(F32), lo.astype(F32)))
    return jnp.where(row < 3, out, 0.0).astype(BF)


def stat_total(own_ref, recv_ref):
    rows = recv_ref[pl.ds(HALF, STAT), :].astype(F32)
    return own_ref[0:1, :] + jnp.sum(rows, axis=0, keepdims=True)


def folded(value):
    return jnp.sum(value.reshape(BS // 8, 8, TOK), axis=0)


def back(index, steps):
    return (index + (4 - steps)) % 4


def blocks(place_ref):
    for sx in range(4):
        xm = back(place_ref[2], sx)
        for sz in range(4):
            zm = back(place_ref[3], sz)
            for ym in range(2):
                yield sx, sz, xm, zm, ym, xm * 8 + zm * 2 + ym


def slot(layer, at, yl):
    return layer * 8 + at * 2 + yl


def rows_of(m):
    return pl.ds(pl.multiple_of(m * BS, BS), BS)


def prep_kernel(place_ref, right_ref, left_ref, gain_ref, keep_ref, send_ref):
    core = place_ref[0]
    for dst, q in ((keep_ref, core), (send_ref, 1 - core)):
        gain_row = gain_ref[q].astype(F32)
        diag = jnp.where(iota2(0) == iota2(1), gain_row, 0.0).astype(BF)
        scaled = mm(diag, right_ref[q]).astype(BF)
        pick = (iota2(0) == column_source(iota2(1), q)).astype(F32).astype(BF)
        dst[0] = mm(scaled, pick).astype(BF)
        pick = (iota2(1) == row_source(iota2(0), q)).astype(F32).astype(BF)
        dst[1] = mm(pick, left_ref[q]).astype(BF)


def taken(pieces, s, k, size, at):
    if s == 2:
        return pieces[2 + k // 2][(k // 2) * (size // 8) + (k % 2) * size + at]
    return pieces[s + s // 3][k * size + at]


def gather_y_kernel(place_ref, p0, p1, p2, p3, right_ref, left_ref):
    core = place_ref[0]
    for s, piece in enumerate((p0, p1, p2, p3)):
        y = back(place_ref[4], s)
        for k in range(2):
            layer = (y // 2) * 2 + (core + k) % 2
            right_ref[layer * 2 + y % 2] = piece[k, 0]
            left_ref[layer * 2 + y % 2] = piece[k, 1]


def gather_pair_kernel(place_ref, *refs):
    for pieces, index, out in ((refs[:5], 3, refs[10]), (refs[5:10], 2, refs[11])):
        for s in range(4):
            at = back(place_ref[index], s)
            for k in range(4):
                for yl in range(2):
                    out[k * 8 + at * 2 + yl] = taken(pieces, s, k, 2, yl)


def tokens_kernel(place_ref, in_ref, cot_ref, x_ref, grad_ref, stat_ref):
    core = place_ref[0]
    base = pl.program_id(0) * BPC
    total = jnp.zeros((8, TOK), F32)
    for i in range(BPC):
        lanes = pl.ds(pl.multiple_of((2 * i + core) * BS, BS), BS)
        x = in_ref[:, :, lanes].reshape(TOK, BS).astype(F32).T
        x_ref[rows_of(base + i), :] = x.astype(BF)
        total = total + folded(x * x)
        grad_ref[rows_of(base + i), :] = cot_ref[:, :, lanes].reshape(TOK, BS).astype(F32).T.astype(BF)
    total = jnp.broadcast_to(jnp.sum(total, axis=0, keepdims=True), (8, TOK))

    @pl.when(pl.program_id(0) == 0)
    def _():
        stat_ref[...] = jnp.zeros_like(stat_ref)

    stat_ref[...] += total


def put_forward(scr, m, product):
    for part in range(2):
        for h in range(2):
            scr[part, pl.ds(m * 2 + h, 32, stride=FORWARD[0]), :] = product[part * 64 + h * 32 :][:32]


def put_backward(scr, m, product):
    for part in range(2):
        scr[part, pl.ds(m, 64, stride=BACKWARD[0]), :] = product[part * 64 :][:64]


def flush(runs, scr, total, own_ref, send_ref, stat_ref):
    pitch, used = runs
    for i in range(HALF // used):
        own_ref[pl.ds(i * used, used), :] = scr[0, pl.ds(i * pitch, used), :].astype(BF)
        send_ref[pl.ds(i * used, used), :] = scr[1, pl.ds(i * pitch, used), :].astype(BF)
    send_ref[pl.ds(HALF, STAT), :] = stat_rows(total)
    stat_ref[...] = jnp.broadcast_to(total, stat_ref.shape)


def gelu_parts(v):
    sq = v * v
    t = jnp.tanh(v * (TANH_SLOPE + (TANH_SLOPE * CUBIC_TERM) * sq))
    half = 0.5 * t + 0.5
    slope = half + (v * (1.0 - t * t)) * (0.5 * TANH_SLOPE + (1.5 * TANH_SLOPE * CUBIC_TERM) * sq)
    return v * half, slope


def rms_of(own_stat, recv_ref):
    return lax.rsqrt(stat_total(own_stat, recv_ref) * (1.0 / D) + EPSILON)


def permuted_block(own_ref, recv_ref, m, rms):
    rows = pl.ds(pl.multiple_of(m * 64, 64), 64)
    both = jnp.concatenate([own_ref[rows, :], recv_ref[rows, :]], axis=0)
    if rms is None:
        return both
    return (both.astype(F32) * rms).astype(BF)


def start_kernel(place_ref, x_ref, st_ref, w0, w1, w2, w3, w4, own_ref, send_ref, stat_ref, scr):
    rights = (w0, w1, w2, w3, w4)
    for sx, sz, xm, zm, ym, m in blocks(place_ref):
        put_forward(scr, m, mm_ta(taken(rights, sx, 0, 8, zm * 2 + ym), x_ref[rows_of(m), :]))
    flush(FORWARD, scr, st_ref[0:1, :], own_ref, send_ref, stat_ref)


def forward_kernel(
    layer, place_ref, uo_ref, ur_ref, us_ref, x_ref, l0, l1, l2, l3, l4, w0, w1, w2, w3, w4,
    xn_ref, slope_ref, perm_ref, rms_ref, own_ref, send_ref, stat_ref, scr,
):
    lefts, rights = (l0, l1, l2, l3, l4), (w0, w1, w2, w3, w4)
    rms = rms_of(us_ref, ur_ref)
    rms_ref[...] = jnp.broadcast_to(rms, rms_ref.shape)
    total = jnp.zeros((8, TOK), F32)
    for sx, sz, xm, zm, ym, m in blocks(place_ref):
        rows = rows_of(m)
        perm = permuted_block(uo_ref, ur_ref, m, rms)
        perm_ref[rows, :] = perm
        value, slope = gelu_parts(mm_ta(taken(lefts, sz, layer, 8, xm * 2 + ym), perm))
        slope_ref[rows, :] = slope.astype(BF)
        xb = (x_ref[rows, :].astype(F32) + value).astype(BF)
        xn_ref[rows, :] = xb
        x = xb.astype(F32)
        total = total + folded(x * x)
        put_forward(scr, m, mm_ta(taken(rights, sx, layer + 1, 8, zm * 2 + ym), xb))
    flush(FORWARD, scr, jnp.sum(total, axis=0, keepdims=True), own_ref, send_ref, stat_ref)


def left_chain(grad, slope, perm, left, rms, m, scr):
    grad_pre = (grad.astype(F32) * slope).astype(BF)
    grad_perm = mm(left, grad_pre)
    put_backward(scr, m, grad_perm * rms)
    return grad_pre, folded(grad_perm * perm.astype(F32))


def turn_kernel(
    layer, place_ref, uo_ref, ur_ref, us_ref, grad_ref, l0, l1, l2, l3, l4,
    rms_ref, perm_ref, pre_ref, own_ref, send_ref, stat_ref, scr,
):
    lefts = (l0, l1, l2, l3, l4)
    rms = rms_of(us_ref, ur_ref)
    rms_ref[...] = jnp.broadcast_to(rms, rms_ref.shape)
    total = jnp.zeros((8, TOK), F32)
    for sx, sz, xm, zm, ym, m in blocks(place_ref):
        rows = rows_of(m)
        perm = permuted_block(uo_ref, ur_ref, m, rms)
        perm_ref[rows, :] = perm
        left = taken(lefts, sz, layer, 8, xm * 2 + ym)
        slope = gelu_parts(mm_ta(left, perm))[1]
        pre_ref[rows, :], add = left_chain(grad_ref[rows, :], slope, perm, left, rms, m, scr)
        total = total + add
    flush(BACKWARD, scr, jnp.sum(total, axis=0, keepdims=True), own_ref, send_ref, stat_ref)


def backward_kernel(layer, *refs):
    place_ref, go_ref, gr_ref, gs_ref, rms_ref, rms_below_ref, x_ref, grad_ref, slope_ref, perm_ref = refs[:10]
    rights, lefts, refs = refs[10:15], refs[15:20], refs[20:]
    pre_ref, own_ref, send_ref, stat_ref = refs[:4]
    new_ref, scr = refs[4] if layer > 1 else None, refs[-1]
    below = layer - 1
    rms = rms_ref[0:1, :]
    rms_below = rms_below_ref[0:1, :]
    coef = stat_total(gs_ref, gr_ref) * (rms * rms * (1.0 / D))
    total = jnp.zeros((8, TOK), F32)
    for sx, sz, xm, zm, ym, m in blocks(place_ref):
        rows = rows_of(m)
        gf = permuted_block(go_ref, gr_ref, m, None)
        grad = grad_ref[rows, :].astype(F32) + mm(taken(rights, sx, layer, 8, zm * 2 + ym), gf)
        grad = (grad - x_ref[rows, :].astype(F32) * coef).astype(BF)
        if new_ref is not None:
            new_ref[rows, :] = grad
        left = taken(lefts, sz, below, 8, xm * 2 + ym)
        pre_ref[rows, :], add = left_chain(
            grad, slope_ref[rows, :].astype(F32), perm_ref[rows, :], left, rms_below, m, scr
        )
        total = total + add
    flush(BACKWARD, scr, jnp.sum(total, axis=0, keepdims=True), own_ref, send_ref, stat_ref)


def factor_kernel(right_layer, left_layer, n_old, *refs):
    refs = refs[n_old:]
    place_ref, refs = refs[0], refs[1:]
    if right_layer is not None:
        (go_ref, gr_ref, x_ref), refs = refs[:3], refs[3:]
    if left_layer is not None:
        (perm_ref, pre_ref), refs = refs[:2], refs[2:]
    for sx, sz, xm, zm, ym, m in blocks(place_ref):
        rows = rows_of(m)
        if right_layer is not None:
            gf = permuted_block(go_ref, gr_ref, m, None)
            refs[sx][slot(right_layer, zm, ym)] = mm_tb(x_ref[rows, :], gf).astype(BF)
        if left_layer is not None:
            refs[sz - 4][slot(left_layer, xm, ym)] = mm_tb(perm_ref[rows, :], pre_ref[rows, :]).astype(BF)


def added(parts):
    parts = [p.astype(F32) for p in parts]
    total = parts[0] + parts[1]
    return total + parts[2] if len(parts) == 3 else total + (parts[2] + parts[3]) if len(parts) == 4 else total


def pass_kernel(place_ref, down_ref, up_ref, lo_ref, hi_ref, down_out, up_out):
    del place_ref
    for i in range(16):
        down_out[i] = added((down_ref[i], lo_ref[i])).astype(BF)
        down_out[16 + i] = down_ref[16 + i]
        up_out[i] = up_ref[i]
        up_out[16 + i] = added((up_ref[16 + i], hi_ref[i])).astype(BF)


def sum_pair_kernel(place_ref, *refs):
    sources, outs = refs[:6], refs[6:]
    for side, index in ((0, 3), (1, 2)):
        slabs = sources[side * 3 :][:3]
        for s in range(4):
            at = back(place_ref[index], s)
            for yl in range(2):
                for layer in range(4):
                    outs[side * 4 + s][yl, layer] = added([t[slot(layer, at, yl)] for t in slabs]).astype(BF)


def sum_ring_kernel(place_ref, *refs):
    sources, outs = refs[:8], refs[8:]
    for side in range(2):
        slabs = sources[side * 4 :][:4]
        for s in range(4):
            y = back(place_ref[4], s)
            for k in range(2):
                outs[s][k, side] = added([t[y % 2, (y // 2) * 2 + k] for t in slabs]).astype(BF)


def sum_y_kernel(place_ref, p0, p1, p2, p3, keep_ref, send_ref):
    core = place_ref[0]
    for dst, k in ((keep_ref, core), (send_ref, 1 - core)):
        for side in range(2):
            dst[side] = added([t[k, side] for t in (p0, p1, p2, p3)])


def finish_kernel(place_ref, keep_ref, recv_ref, right_ref, gain_ref, gr_ref, gl_ref, gg_ref):
    core = place_ref[0]
    for src, q in ((keep_ref, core), (recv_ref, 1 - core)):
        pick = (iota2(1) == column_source(iota2(0), q)).astype(F32)
        raw = mm_exact(src[0], pick)
        diag = jnp.where(iota2(0) == iota2(1), gain_ref[q].astype(F32), 0.0)
        gr_ref[q] = mm_exact(diag, raw)
        gg_ref[q] = mm_exact(jnp.ones((8, BS), F32), raw * right_ref[q].astype(F32), ((1,), (1,)))[0:1]
        pick = (iota2(0) == row_source(iota2(1), q)).astype(F32)
        gl_ref[q] = mm_exact(pick, src[1])


WHOLE = pl.BlockSpec(memory_space=pltpu.VMEM)
SCALARS = pl.BlockSpec(memory_space=pltpu.SMEM)
ANY = pl.BlockSpec(memory_space=pl.ANY)
TOKENS_SPEC = pl.BlockSpec((2, 64, D // GRID), lambda g, place: (place[1], 0, g))


def kept(*shape, dtype=BF):
    return pltpu.VMEM(shape, dtype)


U_OUT = (kept(HALF, TOK), kept(HALF + STAT, TOK), kept(8, TOK, dtype=F32))
ACT = kept(ROWS, TOK)
STATS = kept(8, TOK, dtype=F32)
SLAB = kept(32, BS, BS)
SCRATCH = (pltpu.VMEM((2, HALF + 128, TOK), F32),)


def call(kernel, place, ins, outs, scratch=(), old=()):
    vmem = [pltpu.with_memory_space_constraint(a, pltpu.VMEM) for a in (*old, *ins)]
    ins = (*vmem[: len(old)], place, *vmem[len(old) :])
    return pl.pallas_call(
        kernel,
        out_shape=outs,
        in_specs=[WHOLE] * len(old) + [SCALARS] + [WHOLE] * (len(ins) - len(old) - 1),
        out_specs=(WHOLE,) * len(outs),
        scratch_shapes=scratch,
        compiler_params=pltpu.CompilerParams(vmem_limit_bytes=VMEM_LIMIT),
    )(*ins)


def swapped(value):
    return lax.ppermute(value, "c", SWAP)


def ring(value, axes, steps):
    return lax.ppermute(value, axes, [(i, (i + steps) % 4) for i in range(4)])


def gathered(value, axes):
    return [value] + [ring(value, axes, s) for s in (1, 2, 3)]


def ring_gathered(value, axes):
    half = value.shape[0] // 2
    up, down = ring(value, axes, 1), ring(value, axes, -1)
    spare = half // 16
    return [value, up, ring(up[: half + spare], axes, 1), ring(down[half - spare :], axes, -1), down]


def scattered(slabs, axes):
    return [slabs[0]] + [ring(slabs[s], axes, -s) for s in (1, 2, 3)]


def ring_reduced(right_slabs, left_slabs, place):
    sides = ((right_slabs, "x"), (left_slabs, "z"))
    far = [(ring(slabs[2][:16], axes, -1), ring(slabs[2][16:], axes, 1)) for slabs, axes in sides]
    parts = []
    for (slabs, axes), got in zip(sides, far):
        down, up = call(pass_kernel, place, (slabs[1], slabs[3], *got), (SLAB, SLAB))
        parts += [slabs[0], ring(down, axes, -1), ring(up, axes, 1)]
    return parts


def per_device(inputs, cotangent, right_factor, left_factor, norm_gain):
    core, yh, yl = lax.axis_index("c"), lax.axis_index("yh"), lax.axis_index("yl")
    place = jnp.stack([core, yh, lax.axis_index("x"), lax.axis_index("z"), 2 * yh + yl]).astype(jnp.int32)
    right = right_factor[0]
    left = left_factor[0]
    gain = norm_gain.reshape(2, 1, BS)

    keep, send = pl.pallas_call(
        prep_kernel,
        out_shape=(kept(2, BS, BS),) * 2,
        in_specs=[SCALARS] + [WHOLE] * 3,
        out_specs=(WHOLE,) * 2,
        compiler_params=pltpu.CompilerParams(vmem_limit_bytes=VMEM_LIMIT),
    )(place, right, left, gain)
    mine = jnp.stack([keep, swapped(send)])
    stage = kept(2, 4, BS, BS)
    part = kept(8, BS, BS)
    all_right, all_left = call(gather_y_kernel, place, gathered(mine, YS), (part, part))
    firsts = call(
        gather_pair_kernel, place, ring_gathered(all_right, "z") + ring_gathered(all_left, "x"), (kept(32, BS, BS),) * 2
    )
    rights, lefts = ring_gathered(firsts[0], "x"), ring_gathered(firsts[1], "z")

    x, grad, st = pl.pallas_call(
        tokens_kernel,
        out_shape=(ACT, ACT, STATS),
        grid_spec=pltpu.PrefetchScalarGridSpec(
            num_scalar_prefetch=1, grid=(GRID,), in_specs=[TOKENS_SPEC] * 2, out_specs=(WHOLE,) * 3
        ),
        compiler_params=pltpu.CompilerParams(vmem_limit_bytes=VMEM_LIMIT),
    )(place, inputs, cotangent)

    uo, us, st = call(start_kernel, place, (x, st, *rights), U_OUT, SCRATCH)
    xs, slopes, perms, rmss = [x], [], [], []
    for layer in range(3):
        xn, slope, perm, rms, uo, us, st = call(
            functools.partial(forward_kernel, layer), place,
            (uo, swapped(us), st, xs[-1], *lefts, *rights),
            (ACT, ACT, ACT, STATS) + U_OUT, SCRATCH,
        )
        xs.append(xn)
        slopes.append(slope)
        perms.append(perm)
        rmss.append(rms)
    rms, perm, pre, uo, us, st = call(
        functools.partial(turn_kernel, 3), place, (uo, swapped(us), st, grad, *lefts), (STATS, ACT, ACT) + U_OUT, SCRATCH
    )
    perms.append(perm)
    rmss.append(rms)
    slabs = {"right": (), "left": ()}

    def factors(right_layer, left_layer, ins):
        sides = [side for side, layer in (("right", right_layer), ("left", left_layer)) if layer is not None]
        old, aliases = [], {}
        for n, side in enumerate(sides):
            for k, slab in enumerate(slabs[side]):
                aliases[len(old)] = 4 * n + k
                old.append(slab)
        outs = call_into(
            functools.partial(factor_kernel, right_layer, left_layer, len(old)), place, ins, (SLAB,) * (4 * len(sides)), (), old,
            aliases,
        )
        for n, side in enumerate(sides):
            slabs[side] = outs[4 * n : 4 * n + 4]

    factors(None, 3, (perm, pre))
    for layer in (3, 2, 1):
        below = layer - 1
        go, gr = uo, swapped(us)
        go, slabs["left"] = lax.optimization_barrier((go, slabs["left"]))
        pre, uo, us, st, *grad = call(
            functools.partial(backward_kernel, layer), place,
            (go, gr, st, rmss[layer], rmss[below], xs[layer], *([grad] if layer == 3 else grad), slopes[below], perms[below],
             *rights, *lefts),
            (ACT,) + U_OUT + (ACT,) * (layer > 1), SCRATCH,
        )
        factors(layer, below, (go, gr, xs[layer], perms[below], pre))
    factors(0, None, (uo, swapped(us), xs[0]))
    slabs["right"], slabs["left"] = lax.optimization_barrier((slabs["right"], slabs["left"]))
    outs = call(sum_pair_kernel, place, ring_reduced(slabs["right"], slabs["left"], place), (stage,) * 8)
    parts = scattered(outs[:4], "z") + scattered(outs[4:], "x")
    outs = call(sum_ring_kernel, place, parts, (kept(2, 2, BS, BS),) * 4)
    sums = kept(2, BS, BS, dtype=F32)
    keep, send = call(sum_y_kernel, place, scattered(outs, YS), (sums, sums))
    whole = jax.ShapeDtypeStruct((2, BS, BS), F32)
    grad_right, grad_left, grad_gain = call(
        finish_kernel, place, (keep, swapped(send), right, gain), (whole, whole, jax.ShapeDtypeStruct((2, 1, BS), F32))
    )
    return grad_right[None], grad_left[None], grad_gain.reshape(1, 2 * BS)


def call_into(kernel, place, ins, outs, scratch, old, aliases):
    vmem = [pltpu.with_memory_space_constraint(a, pltpu.VMEM) for a in (*old, *ins)]
    operands = (*vmem[: len(old)], place, *vmem[len(old) :])
    return pl.pallas_call(
        kernel,
        out_shape=outs,
        in_specs=[WHOLE] * len(old) + [SCALARS] + [WHOLE] * len(ins),
        out_specs=(WHOLE,) * len(outs),
        scratch_shapes=scratch,
        input_output_aliases=aliases,
        compiler_params=pltpu.CompilerParams(vmem_limit_bytes=VMEM_LIMIT),
    )(*operands)


def solution(mesh):
    parts = Mesh(mesh.devices.reshape(2, 2, 4, 4, 2), ("yh", "c", "x", "z", "yl"))
    pipe, fsdp = ("yh", "c"), ("x", "z", "yl")
    return jax.shard_map(
        per_device,
        mesh=parts,
        in_specs=(P(None, fsdp, None), P(None, fsdp, None), P(pipe, fsdp, None, None), P(pipe, fsdp, None, None), P(pipe, fsdp)),
        out_specs=(P(pipe, fsdp, None, None), P(pipe, fsdp, None, None), P(pipe, fsdp)),
        check_vma=False,
    )
```
